32 devices in a mesh: rep: 8 (over z, y), fsdp: 4 (over x, core).
Axes of the slice: x: 2, y: 2, z: 4, core: 2. Of those that a mesh axis runs over, the one named last changes fastest.
Arguments:
- query_weights: float32 [8, 4096, 4096], P('rep', 'fsdp'), may hold values from -6 to 6
- key_weights: float32 [8, 4096, 1024], P('rep', 'fsdp'), may hold values from -6 to 6
- value_weights: float32 [8, 4096, 1024], P('rep', 'fsdp'), may hold values from -6 to 6
- query_factor: float32 [8, 4096], replicated, may hold values from -6 to 6
- key_factor: float32 [8, 1024], replicated, may hold values from -6 to 6
- value_factor: float32 [8, 1024], replicated, may hold values from -6 to 6
- step_index: int32 [1], replicated, may hold values from 0 to 63
Outputs:
- query_mixed: float32 [8, 4096, 4096], P('rep', 'fsdp')
- key_mixed: float32 [8, 4096, 1024], P('rep', 'fsdp')
- value_mixed: float32 [8, 4096, 1024], P('rep', 'fsdp')
- query_next: float32 [8, 8, 4096], P('rep')
- key_next: float32 [8, 8, 1024], P('rep')
- value_next: float32 [8, 8, 1024], P('rep')
The draws below stay inside these ranges and needn't reach their ends.
Inputs may be any that keep to these rules, and one draw needn't show every extreme that they name: `step_index`: a non-negative step counter.
All inputs are finite; a program needn't handle non-finite values.
Results may differ from the reference program's by a relative error of at most 0.000071.
Values sent between devices are 32-bit elements; how exact they have to be, the bound alone decides.
No kernel may reach another device: no remote copies, remote signals or barrier semaphores. Data moves between devices by JAX's collectives and lax.ppermute only.
A program may use at most 128 MiB of HBM per device.

```python
import jax
import jax.numpy as jnp
from jax import lax

D = 4096
KV = 1024
RANK = 8
REPLICAS = 8
LEVELS = 3


def levels(rng, shape, shards, smallest, largest):
    def one(position, shards_of):
        heights = jax.random.uniform(jax.random.fold_in(jax.random.fold_in(rng, 6), position), (shards_of,), jnp.float32, smallest / len(shards), largest / len(shards))
        return jnp.repeat(jnp.exp(heights), shape[position] // shards_of).reshape((-1,) + (1,) * (len(shape) - position - 1))

    factor_of = one(*shards[0])
    for cut in shards[1:]:
        factor_of = factor_of * one(*cut)
    return factor_of


def scatter_about(stream_key, extent, spread, limit, cuts=(), held_as=jnp.bfloat16):
    loudness = levels(stream_key, extent, cuts, -0.22, 0.18) if cuts else 1.0
    values = jax.random.normal(stream_key, extent, jnp.float32) * spread * loudness
    return jnp.minimum(jnp.maximum(values, -limit), limit).astype(held_as)


def setup_inputs(seed: int = 0) -> dict:
    streams_of = jax.random.split(jax.random.key(seed), 8)
    query_weights = scatter_about(streams_of[0], (REPLICAS, D, D), 1.0, 6.0, ((0, 8), (1, 4)), jnp.float32)
    key_weights = scatter_about(streams_of[1], (REPLICAS, D, KV), 1.0, 6.0, ((0, 8), (1, 4)), jnp.float32)
    value_weights = scatter_about(streams_of[2], (REPLICAS, D, KV), 1.0, 6.0, ((0, 8), (1, 4)), jnp.float32)
    query_factor = scatter_about(streams_of[3], (RANK, D), 1.0, 6.0, (), jnp.float32)
    key_factor = scatter_about(streams_of[4], (RANK, KV), 1.0, 6.0, (), jnp.float32)
    value_factor = scatter_about(streams_of[5], (RANK, KV), 1.0, 6.0, (), jnp.float32)
    step_index = jax.random.randint(streams_of[6], (1,), 0, 64).astype(jnp.int32)
    return dict(query_weights=query_weights, key_weights=key_weights, value_weights=value_weights, query_factor=query_factor, key_factor=key_factor, value_factor=value_factor, step_index=step_index)


mixing = 0.25
highest = lax.Precision.HIGHEST

def lower_solve(cholesky_factor, values):
    return lax.linalg.triangular_solve(cholesky_factor, values, left_side=True, lower=True)

def normalize(leading):
    grams = jnp.einsum('rkm,rjm->rkj', leading, leading, precision=highest)
    factors = jnp.linalg.cholesky(grams)
    return jax.vmap(lower_solve)(factors, leading)

def apply_update(pieces):
    weights, basis, coeffs = pieces
    return weights - mixing * lax.dot_general(basis, coeffs, (((0,), (0,)), ((), ())), precision=highest)

def gossip(weights, factor, later, earlier):
    images = jnp.einsum('kn,rmn->rkm', factor, weights, precision=highest)
    lead_right = images - images[later]
    lead_left = images[earlier] - images
    basis_right = normalize(lead_right)
    basis_left = normalize(lead_left)
    proj_right = jnp.einsum('rkm,rmn->rkn', basis_right, weights, precision=highest)
    proj_left = jnp.einsum('rkm,rmn->rkn', basis_left, weights, precision=highest)
    next_right = proj_right - proj_left[later]
    next_left = proj_right[earlier] - proj_left
    basis = jnp.concatenate([basis_right, basis_left], axis=1)
    coeffs = jnp.concatenate([next_right, -next_left], axis=1)
    updated = lax.map(apply_update, (weights, basis, coeffs))
    return (updated, next_right)

def reference(query_weights, key_weights, value_weights, query_factor, key_factor, value_factor, step_index):
    level = (step_index[0] % LEVELS).astype(jnp.int32)
    distance = jnp.left_shift(jnp.int32(1), level)
    order = jnp.arange(REPLICAS, dtype=jnp.int32)
    later = ((order + distance) % REPLICAS).astype(jnp.int32)
    earlier = ((order - distance) % REPLICAS).astype(jnp.int32)
    query_mixed, query_next = gossip(query_weights, query_factor, later, earlier)
    key_mixed, key_next = gossip(key_weights, key_factor, later, earlier)
    value_mixed, value_next = gossip(value_weights, value_factor, later, earlier)
    return (query_mixed, key_mixed, value_mixed, query_next, key_next, value_next)
```

```python
import functools

import jax
import jax.numpy as jnp
from jax import lax
from jax.experimental import pallas as pl
from jax.experimental.pallas import tpu as pltpu
from jax.sharding import PartitionSpec as P

mixing = 0.25
F32 = jnp.float32
BF16 = jnp.bfloat16
MIB = 2**20
VMEM = pltpu.VMEM


def vmem_specs(count):
    return [pl.BlockSpec(memory_space=VMEM)] * count


def in_vmem(*arrays):
    return [pltpu.with_memory_space_constraint(array, VMEM) for array in arrays]


def pieces(value):
    high = value.astype(BF16).astype(F32)
    rest = value - high
    middle = rest.astype(BF16).astype(F32)
    return high, middle, rest - middle


def two_pieces(value):
    high = value.astype(BF16)
    return high, (value - high.astype(F32)).astype(BF16)


def weight_dot(stacked, weights, contract):
    high, low = two_pieces(weights)
    dims = (((1,), (contract,)), ((), ()))
    total = lax.dot_general(stacked, high, dims, preferred_element_type=F32)
    total = total + lax.dot_general(stacked, low, dims, preferred_element_type=F32)
    rows = stacked.shape[0] // 3
    return total[:rows] + total[rows : 2 * rows] + total[2 * rows :]


def image_kernel(block_bytes, in_flight, *refs):
    weights, factors = refs[0:3], refs[3:6]
    images, held, sems = refs[6], refs[7:10], refs[10]
    jobs = []
    for family in (1, 2, 0):
        rows, columns = weights[family].shape
        block = min(rows, max(128, block_bytes // (4 * columns)))
        jobs += [(family, start, block) for start in range(0, rows, block)]
    copies = []
    for index, (family, start, block) in enumerate(jobs):
        span = pl.ds(start, block)
        copies.append(
            pltpu.make_async_copy(
                weights[family].at[span], held[family].at[span], sems.at[index % in_flight]
            )
        )
    for copy in copies[:in_flight]:
        copy.start()
    stacks = [jnp.concatenate(pieces(factors[f][...]), axis=0).astype(BF16) for f in range(3)]
    for index, (family, start, block) in enumerate(jobs):
        copies[index].wait()
        if index + in_flight < len(copies):
            copies[index + in_flight].start()
        span = pl.ds(start, block)
        images[pl.ds(8 * family, 8), span] = weight_dot(stacks[family], held[family][span], 1)


def images_of(weights, factors):
    rows = weights[0].shape[0]
    in_flight = 5
    out = pl.pallas_call(
        functools.partial(image_kernel, MIB, in_flight),
        out_shape=(jax.ShapeDtypeStruct((24, rows), F32),)
        + tuple(VMEM(matrix.shape, F32) for matrix in weights),
        in_specs=[pl.BlockSpec(memory_space=pltpu.HBM)] * 3 + vmem_specs(3),
        out_specs=tuple(vmem_specs(4)),
        scratch_shapes=[pltpu.SemaphoreType.DMA((in_flight,))],
        compiler_params=pltpu.CompilerParams(vmem_limit_bytes=12 * MIB),
        name="images",
    )(*[pltpu.with_memory_space_constraint(matrix, pltpu.HBM) for matrix in weights], *factors)
    return out[0], out[1:]


def project_kernel(core_ref, here, before, after, wq, wk, wv, leads, keep, send):
    core = core_ref[0]
    images = here[...]
    right = images - after[...]
    left = before[...] - images
    offset = 0
    weights = (wq, wk, wv)
    grams = []
    for family in range(3):
        rows = slice(8 * family, 8 * family + 8)
        lead = jnp.concatenate([right[rows], left[rows]], axis=0)
        leads[pl.ds(16 * family, 16), :] = lead
        grams.append(
            lax.dot_general(
                lead, lead, (((1,), (1,)), ((), ())), precision=lax.Precision.HIGHEST,
                preferred_element_type=F32,
            )
        )
        stacked = jnp.concatenate(pieces(lead), axis=0).astype(BF16)
        matrix = weights[family]
        half = matrix.shape[1] // 2
        tile = min(half, 512)
        for part in range(2):
            for start in range(0, half, tile):
                product = weight_dot(stacked, matrix[:, pl.ds(part * half + start, tile)], 0)
                span = pl.ds(offset + start, tile)

                @pl.when(core == part)
                def _():
                    keep[:, span] = product

                @pl.when(core != part)
                def _():
                    send[:, span] = product

        offset += half
    gram = jnp.concatenate(grams + [jnp.zeros((16, 80), F32)], axis=1)
    keep[:, pl.ds(offset, 128)] = gram
    send[:, pl.ds(offset, 128)] = gram


def project(core, here, before, after, held):
    rows = here.shape[1]
    width = sum(matrix.shape[1] for matrix in held) // 2 + 128
    return pl.pallas_call(
        project_kernel,
        out_shape=(
            jax.ShapeDtypeStruct((48, rows), F32),
            jax.ShapeDtypeStruct((16, width), F32),
            jax.ShapeDtypeStruct((16, width), F32),
        ),
        in_specs=[pl.BlockSpec(memory_space=pltpu.SMEM)] + vmem_specs(6),
        out_specs=tuple(vmem_specs(3)),
        compiler_params=pltpu.CompilerParams(vmem_limit_bytes=16 * MIB),
        name="project",
    )(core, here, before, after, *in_vmem(*held))


def inverse_cholesky(grams):
    row = lax.broadcasted_iota(jnp.int32, (8, 8), 0)
    unit = (row == lax.broadcasted_iota(jnp.int32, (8, 8), 1)).astype(F32)
    tables = [jnp.concatenate([gram, unit], axis=1) for gram in grams]
    below = lax.broadcasted_iota(jnp.int32, (8, 1), 0)
    for step in range(8):
        after = []
        for table in tables:
            pivot = table[step : step + 1, step : step + 1]
            scale = lax.rsqrt(pivot)
            scale = scale * (1.5 - 0.5 * pivot * scale * scale)
            lead = table[step : step + 1, :] * scale
            factor = table[:, step : step + 1] * scale
            lowered = table - factor * lead
            after.append(jnp.where(below < step, table, jnp.where(below == step, lead, lowered)))
        tables = after
    return [table[:, 8:16] for table in tables]


def apply_rows(matrix, values):
    total = matrix[:, 0:1] * values[0:1, :]
    for index in range(1, 8):
        total = total + matrix[:, index : index + 1] * values[index : index + 1, :]
    return total


def update_kernel(
    slots, core_ref, leads, mine, other, wq, wk, wv, mq, mk, mv, nq, nk, nv, stage, basis_ref, coeff_ref, sems
):
    core = core_ref[0]
    weights, mixed, following = (wq, wk, wv), (mq, mk, mv), (nq, nk, nv)
    width = mine.shape[1] - 128
    sums = mine[:, width : width + 128]
    grams = []
    for family in range(3):
        grams.append(sums[0:8, 16 * family : 16 * family + 8])
        grams.append(sums[8:16, 16 * family + 8 : 16 * family + 16])
    solved = inverse_cholesky(grams)
    copies = []
    offset = 0
    for family in range(3):
        right, left = solved[2 * family], solved[2 * family + 1]
        lead = leads[pl.ds(16 * family, 16), :]
        basis = jnp.concatenate([apply_rows(right, lead[0:8]), apply_rows(left, lead[8:16])], axis=0)
        high, middle, low = pieces(basis)
        basis_ref[family] = jnp.concatenate([high, high, high, middle, middle, low], axis=0).astype(BF16)
        half = weights[family].shape[1] // 2
        for part in range(2):
            chosen = core == part
            span = slice(offset, offset + half)
            sums_here = jnp.where(chosen, mine[:, span], other[:, span])
            next_right = apply_rows(right, sums_here[0:8])
            next_left = apply_rows(left, sums_here[8:16])
            following[family][:, pl.ds(part * half, half)] = next_right
            coeff = jnp.concatenate([next_right, -next_left], axis=0)
            high, middle, low = pieces(coeff)
            coeff_ref[:, pl.ds(2 * offset + part * half, half)] = jnp.concatenate(
                [high, middle, low, high, middle, high], axis=0
            ).astype(BF16)
        offset += half
    offset = 0
    count = 0
    for family in range(3):
        rows, columns = weights[family].shape
        tile, block = min(columns, stage.shape[2]), min(rows, stage.shape[1])
        for column in range(0, columns, tile):
            for start in range(0, rows, block):
                slot = count % slots
                if count >= slots:
                    copies[count - slots].wait()
                change = lax.dot_general(
                    basis_ref[family, :, pl.ds(start, block)],
                    coeff_ref[:, pl.ds(offset + column, tile)],
                    (((0,), (0,)), ((), ())),
                    preferred_element_type=F32,
                )
                place = (pl.ds(start, block), pl.ds(column, tile))
                stage[slot] = weights[family][place] - mixing * change
                copy = pltpu.make_async_copy(stage.at[slot], mixed[family].at[place], sems.at[slot])
                copy.start()
                copies.append(copy)
                count += 1
        offset += columns
    for copy in copies[-slots:]:
        copy.wait()


def update(core, leads, mine, other, held):
    rows = held[0].shape[0]
    columns = sum(matrix.shape[1] for matrix in held)
    slots = 4
    block = min(256, rows)
    return pl.pallas_call(
        functools.partial(update_kernel, slots),
        out_shape=tuple(jax.ShapeDtypeStruct(matrix.shape, F32) for matrix in held)
        + tuple(jax.ShapeDtypeStruct((8, matrix.shape[1]), F32) for matrix in held),
        in_specs=[pl.BlockSpec(memory_space=pltpu.SMEM)] + vmem_specs(6),
        out_specs=tuple([pl.BlockSpec(memory_space=pl.ANY)] * 3 + vmem_specs(3)),
        scratch_shapes=[
            VMEM((slots, block, 1024), F32),
            VMEM((3, 96, rows), BF16),
            VMEM((96, columns), BF16),
            pltpu.SemaphoreType.DMA((slots,)),
        ],
        compiler_params=pltpu.CompilerParams(vmem_limit_bytes=16 * MIB),
        name="update",
    )(core, leads, mine, other, *in_vmem(*held))


def moved(value, axis, target):
    count = lax.axis_size(axis)
    return lax.ppermute(value, axis, [(source, target(source, count)) for source in range(count)])


def along(value, distance):
    return moved(value, "rep", lambda source, count: (source + distance) % count)


def swapped(value, bit):
    return moved(value, "fsdp", lambda source, count: source ^ bit)


def one_round(distance, operands):
    weights, factors, core = operands
    images, held = images_of(weights, factors)
    before, after = along(images, distance), along(images, -distance)
    leads, keep, send = project(core, images, before, after, held)
    total = keep + swapped(send, 1)
    width = total.shape[1] - 128
    right, left = total[0:8, :width], total[8:16, :width]
    right_before, left_after = along(right, distance), along(left, -distance)
    sums = jnp.concatenate([right - left_after, right_before - left], axis=0)
    sums = jnp.concatenate([sums, total[:, width:]], axis=1)
    bit = 2
    while bit < lax.axis_size("fsdp"):
        sums = sums + swapped(sums, bit)
        bit *= 2
    other = swapped(sums[:, :width], 1)
    return update(core, leads, sums, other, held)


def per_device(query_weights, key_weights, value_weights, query_factor, key_factor, value_factor, step_index):
    weights = (query_weights[0], key_weights[0], value_weights[0])
    factors = (query_factor, key_factor, value_factor)
    core = (lax.axis_index("fsdp") % 2).astype(jnp.int32).reshape(1)
    levels = lax.axis_size("rep").bit_length() - 1
    branches = [functools.partial(one_round, 1 << level) for level in range(levels)]
    outs = lax.switch(step_index[0] % levels, branches, (weights, factors, core))
    return tuple(out[None] for out in outs)


def solution(mesh):
    split = P("rep", "fsdp", None)
    return jax.shard_map(
        per_device,
        mesh=mesh,
        in_specs=(split, split, split, P(), P(), P(), P()),
        out_specs=(split, split, split) + (P("rep", None, None),) * 3,
        check_vma=False,
    )
```

```python
import functools

import jax
import jax.numpy as jnp
from jax import lax
from jax.experimental import pallas as pl
from jax.experimental.pallas import tpu as pltpu
from jax.sharding import PartitionSpec as P

mixing = 0.25
F32 = jnp.float32
BF16 = jnp.bfloat16
MIB = 2**20
VMEM = pltpu.VMEM


def vmem_specs(count):
    return [pl.BlockSpec(memory_space=VMEM)] * count


def in_vmem(*arrays):
    return [pltpu.with_memory_space_constraint(array, VMEM) for array in arrays]


def pieces(value):
    high = value.astype(BF16).astype(F32)
    rest = value - high
    middle = rest.astype(BF16).astype(F32)
    return high, middle, rest - middle


def two_pieces(value):
    high = value.astype(BF16)
    return high, (value - high.astype(F32)).astype(BF16)


def weight_dot(stacked, weights, contract):
    high, low = two_pieces(weights)
    dims = (((1,), (contract,)), ((), ()))
    total = lax.dot_general(stacked, high, dims, preferred_element_type=F32)
    total = total + lax.dot_general(stacked, low, dims, preferred_element_type=F32)
    rows = stacked.shape[0] // 3
    return total[:rows] + total[rows : 2 * rows] + total[2 * rows :]


def image_kernel(in_flight, *refs):
    weights, factors = refs[0:3], refs[3:6]
    images, held, stack_ref, sems = refs[6], refs[7:10], refs[10], refs[11]
    rows = weights[0].shape[0]
    block = min(rows, 256)
    blocks = rows // block
    tile = min(matrix.shape[1] for matrix in weights)
    jobs = []
    for family in (1, 2, 0):
        for column in range(0, weights[family].shape[1], tile):
            jobs.append((family, column))
    offsets, offset = [], 0
    for family in range(3):
        offsets.append(offset)
        offset += weights[family].shape[1]

    def copy_of(job, index):
        family, column = jobs[job]
        place = (pl.ds(pl.multiple_of(index * block, block), block), pl.ds(column, tile))
        return pltpu.make_async_copy(
            weights[family].at[place], held[family].at[place], sems.at[job * blocks + index]
        )

    ahead = in_flight // blocks
    for job in range(min(ahead, len(jobs))):
        for index in range(blocks):
            copy_of(job, index).start()
    for family in range(3):
        columns = weights[family].shape[1]
        stack_ref[:, pl.ds(offsets[family], columns)] = jnp.concatenate(
            pieces(factors[family][...]), axis=0
        ).astype(BF16)
    for job, (family, column) in enumerate(jobs):
        stack = stack_ref[:, pl.ds(offsets[family] + column, tile)]
        wide = pl.ds(column, tile)

        def step(index, carry):
            copy_of(job, index).wait()
            if job + ahead < len(jobs):
                copy_of(job + ahead, index).start()
            span = pl.ds(pl.multiple_of(index * block, block), block)
            part = weight_dot(stack, held[family][span, wide], 1)
            here = pl.ds(8 * family, 8)
            if column == 0:
                images[here, span] = part
            else:
                images[here, span] += part
            return carry

        lax.fori_loop(0, blocks, step, 0)


def images_of(weights, factors):
    rows = weights[0].shape[0]
    columns = sum(matrix.shape[1] for matrix in weights)
    in_flight = 8
    tile = min(matrix.shape[1] for matrix in weights)
    copies = (columns // tile) * (rows // min(rows, 256))
    out = pl.pallas_call(
        functools.partial(image_kernel, in_flight),
        out_shape=(jax.ShapeDtypeStruct((24, rows), F32),)
        + tuple(VMEM(matrix.shape, F32) for matrix in weights),
        in_specs=[pl.BlockSpec(memory_space=pltpu.HBM)] * 3 + vmem_specs(3),
        out_specs=tuple(vmem_specs(4)),
        scratch_shapes=[VMEM((24, columns), BF16), pltpu.SemaphoreType.DMA((copies,))],
        compiler_params=pltpu.CompilerParams(vmem_limit_bytes=8 * MIB),
        name="images",
    )(*[pltpu.with_memory_space_constraint(matrix, pltpu.HBM) for matrix in weights], *factors)
    return out[0], out[1:]


def project_kernel(here, before, after, wq, wk, wv, leads, keep, send):
    core = lax.rem(lax.axis_index("fsdp"), 2)
    images = here[...]
    right = images - after[...]
    left = before[...] - images
    offset = 0
    weights = (wq, wk, wv)
    grams = []
    for family in range(3):
        rows = slice(8 * family, 8 * family + 8)
        lead = jnp.concatenate([right[rows], left[rows]], axis=0)
        leads[pl.ds(16 * family, 16), :] = lead
        grams.append(
            lax.dot_general(
                lead, lead, (((1,), (1,)), ((), ())), precision=lax.Precision.HIGHEST,
                preferred_element_type=F32,
            )
        )
        stacked = jnp.concatenate(pieces(lead), axis=0).astype(BF16)
        matrix = weights[family]
        half = matrix.shape[1] // 2
        tile = min(half, 512)
        for part in range(2):
            for start in range(0, half, tile):
                product = weight_dot(stacked, matrix[:, pl.ds(part * half + start, tile)], 0)
                span = pl.ds(offset + start, tile)

                @pl.when(core == part)
                def _():
                    keep[:, span] = product

                @pl.when(core != part)
                def _():
                    send[:, span] = product

        offset += half
    gram = jnp.concatenate(grams + [jnp.zeros((16, 80), F32)], axis=1)
    keep[:, pl.ds(offset, 128)] = gram
    send[:, pl.ds(offset, 128)] = gram


def project(here, before, after, held):
    rows = here.shape[1]
    width = sum(matrix.shape[1] for matrix in held) // 2 + 128
    return pl.pallas_call(
        project_kernel,
        out_shape=(
            jax.ShapeDtypeStruct((48, rows), F32),
            jax.ShapeDtypeStruct((16, width), F32),
            jax.ShapeDtypeStruct((16, width), F32),
        ),
        in_specs=vmem_specs(6),
        out_specs=tuple(vmem_specs(3)),
        compiler_params=pltpu.CompilerParams(vmem_limit_bytes=10 * MIB),
        name="project",
    )(here, before, after, *in_vmem(*held))


def inverse_cholesky(grams):
    row = lax.broadcasted_iota(jnp.int32, (8, 8), 0)
    unit = (row == lax.broadcasted_iota(jnp.int32, (8, 8), 1)).astype(F32)
    tables = [jnp.concatenate([gram, unit], axis=1) for gram in grams]
    below = lax.broadcasted_iota(jnp.int32, (8, 1), 0)
    for step in range(8):
        after = []
        for table in tables:
            pivot = table[step : step + 1, step : step + 1]
            scale = lax.rsqrt(pivot)
            scale = scale * (1.5 - 0.5 * pivot * scale * scale)
            lead = table[step : step + 1, :] * scale
            factor = table[:, step : step + 1] * scale
            lowered = table - factor * lead
            after.append(jnp.where(below < step, table, jnp.where(below == step, lead, lowered)))
        tables = after
    return [table[:, 8:16] for table in tables]


def apply_rows(matrix, values):
    total = matrix[:, 0:1] * values[0:1, :]
    for index in range(1, 8):
        total = total + matrix[:, index : index + 1] * values[index : index + 1, :]
    return total


def update_kernel(
    slots, leads, mine, other, wq, wk, wv, mq, mk, mv, nq, nk, nv, stage, basis_ref, coeff_ref, sems
):
    core = lax.rem(lax.axis_index("fsdp"), 2)
    weights, mixed, following = (wq, wk, wv), (mq, mk, mv), (nq, nk, nv)
    width = mine.shape[1] - 128
    sums = mine[:, width : width + 128]
    grams = []
    for family in range(3):
        grams.append(sums[0:8, 16 * family : 16 * family + 8])
        grams.append(sums[8:16, 16 * family + 8 : 16 * family + 16])
    solved = inverse_cholesky(grams)
    copies = []
    offset = 0
    for family in range(3):
        right, left = solved[2 * family], solved[2 * family + 1]
        lead = leads[pl.ds(16 * family, 16), :]
        basis = jnp.concatenate([apply_rows(right, lead[0:8]), apply_rows(left, lead[8:16])], axis=0)
        high, middle, low = pieces(basis)
        basis_ref[family] = jnp.concatenate([high, high, high, middle, middle, low], axis=0).astype(BF16)
        half = weights[family].shape[1] // 2
        for part in range(2):
            chosen = core == part
            span = slice(offset, offset + half)
            sums_here = jnp.where(chosen, mine[:, span], other[:, span])
            next_right = apply_rows(right, sums_here[0:8])
            next_left = apply_rows(left, sums_here[8:16])
            following[family][0, :, pl.ds(part * half, half)] = next_right
            coeff = jnp.concatenate([next_right, -next_left], axis=0)
            high, middle, low = pieces(coeff)
            coeff_ref[:, pl.ds(2 * offset + part * half, half)] = jnp.concatenate(
                [high, middle, low, high, middle, high], axis=0
            ).astype(BF16)
        offset += half
    offset = 0
    count = 0
    for family in range(3):
        rows, columns = weights[family].shape
        tile, block = min(columns, stage.shape[2]), min(rows, stage.shape[1])
        for column in range(0, columns, tile):
            for start in range(0, rows, block):
                slot = count % slots
                if count >= slots:
                    copies[count - slots].wait()
                change = lax.dot_general(
                    basis_ref[family, :, pl.ds(start, block)],
                    coeff_ref[:, pl.ds(offset + column, tile)],
                    (((0,), (0,)), ((), ())),
                    preferred_element_type=F32,
                )
                place = (pl.ds(start, block), pl.ds(column, tile))
                stage[slot] = weights[family][place] - mixing * change
                copy = pltpu.make_async_copy(stage.at[slot], mixed[family].at[(0,) + place], sems.at[slot])
                copy.start()
                copies.append(copy)
                count += 1
        offset += columns
    for copy in copies[-slots:]:
        copy.wait()


def update(leads, mine, other, held):
    rows = held[0].shape[0]
    columns = sum(matrix.shape[1] for matrix in held)
    slots = 4
    block = min(256, rows)
    return pl.pallas_call(
        functools.partial(update_kernel, slots),
        out_shape=tuple(pltpu.HBM((1,) + matrix.shape, F32) for matrix in held)
        + tuple(jax.ShapeDtypeStruct((1, 8, matrix.shape[1]), F32) for matrix in held),
        in_specs=vmem_specs(6),
        out_specs=tuple([pl.BlockSpec(memory_space=pltpu.HBM)] * 3 + vmem_specs(3)),
        scratch_shapes=[
            VMEM((slots, block, 1024), F32),
            VMEM((3, 96, rows), BF16),
            VMEM((96, columns), BF16),
            pltpu.SemaphoreType.DMA((slots,)),
        ],
        compiler_params=pltpu.CompilerParams(vmem_limit_bytes=10 * MIB),
        name="update",
    )(leads, mine, other, *in_vmem(*held))


def moved(value, axis, target):
    count = lax.axis_size(axis)
    return lax.ppermute(value, axis, [(source, target(source, count)) for source in range(count)])


def along(value, distance):
    return moved(value, "rep", lambda source, count: (source + distance) % count)


def swapped(value, bit):
    return moved(value, "fsdp", lambda source, count: source ^ bit)


def one_round(distance, images, held):
    before, after = along(images, distance), along(images, -distance)
    leads, keep, send = project(images, before, after, held)
    total = keep + swapped(send, 1)
    width = total.shape[1] - 128
    right, left = total[0:8, :width], total[8:16, :width]
    right_before, left_after = along(right, distance), along(left, -distance)
    sums = jnp.concatenate([right - left_after, right_before - left], axis=0)
    sums = jnp.concatenate([sums, total[:, width:]], axis=1)
    bit = 2
    while bit < lax.axis_size("fsdp"):
        sums = sums + swapped(sums, bit)
        bit *= 2
    other = swapped(sums[:, :width], 1)
    return update(leads, sums, other, held)


def per_device(query_weights, key_weights, value_weights, query_factor, key_factor, value_factor, step_index):
    weights = (query_weights[0], key_weights[0], value_weights[0])
    factors = (query_factor, key_factor, value_factor)
    levels = lax.axis_size("rep").bit_length() - 1
    images, held = images_of(weights, factors)
    branches = [functools.partial(one_round, 1 << level) for level in range(levels)]
    return lax.switch(step_index[0] % levels, branches, images, held)


def solution(mesh):
    split = P("rep", "fsdp", None)
    return jax.shard_map(
        per_device,
        mesh=mesh,
        in_specs=(split, split, split, P(), P(), P(), P()),
        out_specs=(split, split, split) + (P("rep", None, None),) * 3,
        check_vma=False,
    )
```

```python
import functools

import jax
import jax.numpy as jnp
from jax import lax
from jax.experimental import pallas as pl
from jax.experimental.pallas import tpu as pltpu
from jax.sharding import PartitionSpec as P

mixing = 0.25
F32 = jnp.float32
BF16 = jnp.bfloat16
MIB = 2**20
VMEM = pltpu.VMEM
RANK = 8


def vmem_specs(count):
    return [pl.BlockSpec(memory_space=VMEM)] * count


def hbm_specs(count):
    return [pl.BlockSpec(memory_space=pltpu.HBM)] * count


def in_vmem(*arrays):
    return [pltpu.with_memory_space_constraint(array, VMEM) for array in arrays]


def in_hbm(*arrays):
    return [pltpu.with_memory_space_constraint(array, pltpu.HBM) for array in arrays]


def cost(size, rows):
    return pl.CostEstimate(flops=2 * size * rows, bytes_accessed=4 * size, transcendentals=0)


def pieces(value):
    high = value.astype(BF16).astype(F32)
    rest = value - high
    middle = rest.astype(BF16).astype(F32)
    return high, middle, rest - middle


def stack_of(value):
    return jnp.concatenate(pieces(value), axis=0).astype(BF16)


def weight_dot(stacked, weights, contract):
    high = weights.astype(BF16)
    low = (weights - high.astype(F32)).astype(BF16)
    dims = (((1,), (contract,)), ((), ()))
    total = lax.dot_general(stacked, high, dims, preferred_element_type=F32)
    total = total + lax.dot_general(stacked, low, dims, preferred_element_type=F32)
    rows = stacked.shape[0] // 3
    return total[:rows] + total[rows : 2 * rows] + total[2 * rows :]


def family_of(tile, tiles):
    family, place, start = 0, tile, 0
    for count in tiles[:-1]:
        start += count
        family = family + jnp.where(tile >= start, 1, 0)
        place = jnp.where(tile >= start, tile - start, place)
    return family, place


def image_kernel(tiles, tile, block, in_flight, *refs):
    weights, factors = refs[:3], refs[3:6]
    images, held = refs[6:8]
    brought, stack_ref, sems, factor_sems = refs[8:11], refs[11], refs[12], refs[13]
    rows = held.shape[0]
    blocks = rows // block
    jobs = sum(tiles) * blocks

    def copy_of(family, place, job):
        start, wide = (job % blocks) * block, (job // blocks) * tile
        column = place * tile
        if not isinstance(job, int):
            start, wide = pl.multiple_of(start, block), pl.multiple_of(wide, tile)
            column = pl.multiple_of(column, tile)
        span = pl.ds(start, block)
        return pltpu.make_async_copy(
            weights[family].at[span, pl.ds(column, tile)],
            held.at[span, pl.ds(wide, tile)],
            sems.at[job % in_flight],
        )

    for job in range(min(jobs, in_flight)):
        copy_of(0, job // blocks, job).start()
    factor_copies = [
        pltpu.make_async_copy(factors[family], brought[family], factor_sems.at[family])
        for family in range(3)
    ]
    for copy in factor_copies:
        copy.start()
    offset = 0
    for family in range(3):
        columns = tiles[family] * tile
        factor_copies[family].wait()
        stack_ref[:, pl.ds(offset, columns)] = stack_of(brought[family][...])
        offset += columns
    images[...] = jnp.zeros_like(images)

    def step(job, carry):
        copy_of(0, 0, job).wait()
        following = job + in_flight
        later, place = family_of(following // blocks, tiles)
        for family in range(3):

            @pl.when((later == family) & (following < jobs))
            def _():
                copy_of(family, place, following).start()

        span = pl.ds(pl.multiple_of((job % blocks) * block, block), block)
        wide = pl.ds(pl.multiple_of((job // blocks) * tile, tile), tile)
        part = weight_dot(stack_ref[:, wide], held[span, wide], 1)
        family, _ = family_of(job // blocks, tiles)
        images[pl.ds(pl.multiple_of(RANK * family, RANK), RANK), span] += part
        return carry

    lax.fori_loop(0, jobs, step, 0)


def images_of(weights, factors, tiles, tile):
    rows = weights[0].shape[0]
    columns = sum(tiles) * tile
    block = min(rows, 512)
    in_flight = min(3, tiles[0] * (rows // block))
    return pl.pallas_call(
        functools.partial(image_kernel, tiles, tile, block, in_flight),
        out_shape=(jax.ShapeDtypeStruct((3 * RANK, rows), F32), VMEM((rows, columns), F32)),
        in_specs=hbm_specs(6),
        out_specs=tuple(vmem_specs(2)),
        scratch_shapes=[VMEM(factor.shape, F32) for factor in factors]
        + [
            VMEM((3 * RANK, columns), BF16),
            pltpu.SemaphoreType.DMA((in_flight,)),
            pltpu.SemaphoreType.DMA((3,)),
        ],
        compiler_params=pltpu.CompilerParams(vmem_limit_bytes=8 * MIB),
        cost_estimate=cost(rows * columns, RANK),
        name="images",
    )(*in_hbm(*weights, *factors))


def project_kernel(sides, tiles, tile, here, after, before, held, leads, keep, send, stack_ref):
    core = lax.rem(lax.axis_index("fsdp"), 2)
    images = here[...]
    right = images - after[...]
    left = before[...] - images
    rows = RANK * sides
    grams = []
    for family in range(3):
        mine = slice(RANK * family, RANK * family + RANK)
        lead = right[mine] if sides == 1 else jnp.concatenate([right[mine], left[mine]], axis=0)
        leads[pl.ds(rows * family, rows), :] = lead
        stack_ref[family] = stack_of(lead)
        grams.append(
            lax.dot_general(
                lead,
                lead,
                (((1,), (1,)), ((), ())),
                precision=lax.Precision.HIGHEST,
                preferred_element_type=F32,
            )
        )
    gram = jnp.concatenate(grams + [jnp.zeros((rows, 128 - 3 * rows), F32)], axis=1)
    keep[:, pl.ds(0, 128)] = gram
    send[:, pl.ds(0, 128)] = gram
    half = sum(tiles) // 2

    def step(index, carry):
        family, _ = family_of(index, tiles)
        product = weight_dot(stack_ref[family], held[:, pl.ds(pl.multiple_of(index * tile, tile), tile)], 0)
        span = pl.ds(pl.multiple_of(128 + (index % half) * tile, 128), tile)

        @pl.when(core == index // half)
        def _():
            keep[:, span] = product

        @pl.when(core != index // half)
        def _():
            send[:, span] = product

        return carry

    lax.fori_loop(0, 2 * half, step, 0)


def project(sides, tiles, tile, here, after, before, held):
    rows = RANK * sides
    width = held.shape[1] // 2 + 128
    return pl.pallas_call(
        functools.partial(project_kernel, sides, tiles, tile),
        out_shape=(
            jax.ShapeDtypeStruct((3 * rows, here.shape[1]), F32),
            jax.ShapeDtypeStruct((rows, width), F32),
            jax.ShapeDtypeStruct((rows, width), F32),
        ),
        in_specs=vmem_specs(4),
        out_specs=tuple(vmem_specs(3)),
        scratch_shapes=[VMEM((3, 3 * rows, here.shape[1]), BF16)],
        compiler_params=pltpu.CompilerParams(vmem_limit_bytes=12 * MIB),
        cost_estimate=cost(held.size, 2 * RANK),
        name="project",
    )(here, after, before, *in_vmem(held))


def inverse_cholesky(grams):
    shape = (RANK, RANK)
    row = lax.broadcasted_iota(jnp.int32, shape, 0)
    unit = (row == lax.broadcasted_iota(jnp.int32, shape, 1)).astype(F32)
    tables = [jnp.concatenate([gram, unit], axis=1) for gram in grams]
    below = lax.broadcasted_iota(jnp.int32, (RANK, 1), 0)
    for step in range(RANK):
        after = []
        for table in tables:
            pivot = table[step : step + 1, step : step + 1]
            scale = lax.rsqrt(pivot)
            scale = scale * (1.5 - 0.5 * pivot * scale * scale)
            lead = table[step : step + 1, :] * scale
            factor = table[:, step : step + 1] * scale
            lowered = table - factor * lead
            after.append(jnp.where(below < step, table, jnp.where(below == step, lead, lowered)))
        tables = after
    return [table[:, RANK:] for table in tables]


def apply_rows(matrix, values):
    total = matrix[:, 0:1] * values[0:1, :]
    for index in range(1, RANK):
        total = total + matrix[:, index : index + 1] * values[index : index + 1, :]
    return total


def normalise_kernel(sides, grams, leads, inverses, bases):
    rows = RANK * sides
    tables = []
    for family in range(3):
        for side in range(sides):
            span = slice(RANK * side, RANK * side + RANK)
            start = rows * family + RANK * side
            tables.append(grams[span, start : start + RANK])
    solved = inverse_cholesky(tables)
    for family in range(3):
        basis = []
        for side in range(sides):
            inverse = solved[sides * family + side]
            inverses[family, side] = inverse
            basis.append(apply_rows(inverse, leads[pl.ds(rows * family + RANK * side, RANK), :]))
        high, middle, low = pieces(jnp.concatenate(basis, axis=0) if sides > 1 else basis[0])
        bases[family] = jnp.concatenate([high, high, high, middle, middle, low], axis=0).astype(BF16)


def normalise(sides, grams, leads):
    rows = RANK * sides
    return pl.pallas_call(
        functools.partial(normalise_kernel, sides),
        out_shape=(
            jax.ShapeDtypeStruct((3, sides, RANK, RANK), F32),
            jax.ShapeDtypeStruct((3, 6 * rows, leads.shape[1]), BF16),
        ),
        in_specs=vmem_specs(2),
        out_specs=tuple(vmem_specs(2)),
        compiler_params=pltpu.CompilerParams(vmem_limit_bytes=4 * MIB),
        cost_estimate=pl.CostEstimate(flops=10**6, bytes_accessed=4 * MIB, transcendentals=48),
        name="normalise",
    )(grams, leads)


def update_kernel(sides, tiles, slots, inverses, bases, mine, other, held, *refs):
    mixed, following = refs[:3], refs[3:6]
    stage, coeff_ref, sems = refs[6:]
    core = lax.rem(lax.axis_index("fsdp"), 2)
    block, tile = stage.shape[1:]
    blocks = held.shape[0] // block
    half = sum(tiles) // 2
    factor = mixing * (2 // sides)

    def copy_of(family, place, job, slot):
        start = pl.multiple_of((job % blocks) * block, block)
        column = pl.multiple_of(place * tile, tile)
        target = mixed[family].at[0, pl.ds(start, block), pl.ds(column, tile)]
        return pltpu.make_async_copy(stage.at[slot], target, sems.at[slot])

    def change(job, carry):
        slot = job % slots
        index = job // blocks
        family, place = family_of(index, tiles)

        @pl.when(job % blocks == 0)
        def _():
            span = pl.ds(pl.multiple_of((index % half) * tile, tile), tile)
            chosen = jnp.where(core == index // half, mine[:, span], other[:, span])
            renewed = [
                apply_rows(inverses[family, side], chosen[RANK * side : RANK * side + RANK])
                for side in range(sides)
            ]
            for which in range(3):

                @pl.when(family == which)
                def _():
                    following[which][0, :, pl.ds(pl.multiple_of(place * tile, tile), tile)] = renewed[0]

            coeff = renewed[0] if sides == 1 else jnp.concatenate([renewed[0], -renewed[1]], axis=0)
            high, middle, low = pieces(coeff)
            coeff_ref[...] = jnp.concatenate([high, middle, low, high, middle, high], axis=0).astype(BF16)

        @pl.when(job >= slots)
        def _():
            copy_of(0, 0, 0, slot).wait()

        span = pl.ds(pl.multiple_of((job % blocks) * block, block), block)
        product = lax.dot_general(
            bases[family, :, span],
            coeff_ref[...],
            (((0,), (0,)), ((), ())),
            preferred_element_type=F32,
        )
        stage[slot] = held[span, pl.ds(pl.multiple_of(index * tile, tile), tile)] - factor * product
        for which in range(3):

            @pl.when(family == which)
            def _():
                copy_of(which, place, job, slot).start()

        return carry

    jobs = blocks * sum(tiles)
    lax.fori_loop(0, jobs, change, 0)
    for slot in range(min(slots, jobs)):
        copy_of(0, 0, 0, slot).wait()


def update(sides, tiles, tile, inverses, bases, mine, other, held):
    rows = held.shape[0]
    slots = 3
    return pl.pallas_call(
        functools.partial(update_kernel, sides, tiles, slots),
        out_shape=tuple(pltpu.HBM((1, rows, count * tile), F32) for count in tiles)
        + tuple(jax.ShapeDtypeStruct((1, RANK, count * tile), F32) for count in tiles),
        in_specs=vmem_specs(5),
        out_specs=tuple(hbm_specs(3) + vmem_specs(3)),
        scratch_shapes=[
            VMEM((slots, min(512, rows), tile), F32),
            VMEM((6 * RANK * sides, tile), BF16),
            pltpu.SemaphoreType.DMA((slots,)),
        ],
        compiler_params=pltpu.CompilerParams(vmem_limit_bytes=12 * MIB),
        cost_estimate=cost(held.size, 2 * RANK),
        name="update",
    )(inverses, bases, mine, other, *in_vmem(held))


def moved(value, axis, target):
    count = lax.axis_size(axis)
    return lax.ppermute(value, axis, [(source, target(source, count)) for source in range(count)])


def along(value, distance):
    return moved(value, "rep", lambda source, count: (source + distance) % count)


def swapped(value, bit):
    return moved(value, "fsdp", lambda source, count: source ^ bit)


def summed(value):
    bit = 2
    while bit < lax.axis_size("fsdp"):
        value = value + swapped(value, bit)
        bit *= 2
    return value


def differences(distance, sides, values):
    right = values[:RANK]
    if sides == 1:
        return right + along(right, distance)
    left = values[RANK:]
    return jnp.concatenate([right - along(left, -distance), along(right, distance) - left], axis=0)


def one_round(tiles, tile, distance, images, held):
    sides = 1 if 2 * distance == lax.axis_size("rep") else 2
    after = along(images, -distance)
    before = after if sides == 1 else along(images, distance)
    leads, keep, send = project(sides, tiles, tile, images, after, before, held)
    total = keep + swapped(send, 1)
    parts = differences(distance, sides, total[:, 128:])
    parts = summed(jnp.concatenate([total[:, :128], parts], axis=1))
    mine = parts[:, 128:]
    other = swapped(mine, 1)
    inverses, bases = normalise(sides, parts[:, :128], leads)
    return update(sides, tiles, tile, inverses, bases, mine, other, held)


def per_device(query_weights, key_weights, value_weights, query_factor, key_factor, value_factor, step_index):
    weights = (query_weights[0], key_weights[0], value_weights[0])
    levels = lax.axis_size("rep").bit_length() - 1
    tile = min(1024, *[matrix.shape[1] for matrix in weights])
    tiles = tuple(matrix.shape[1] // tile for matrix in weights)
    images, held = images_of(weights, (query_factor, key_factor, value_factor), tiles, tile)
    branches = [functools.partial(one_round, tiles, tile, 1 << level) for level in range(levels)]
    return lax.switch(step_index[0] % levels, branches, images, held)


def solution(mesh):
    split = P("rep", "fsdp", None)
    return jax.shard_map(
        per_device,
        mesh=mesh,
        in_specs=(split, split, split, P(), P(), P(), P()),
        out_specs=(split, split, split) + (P("rep", None, None),) * 3,
        check_vma=False,
    )
```

```python
import functools

import jax
import jax.numpy as jnp
from jax import lax
from jax.experimental import pallas as pl
from jax.experimental.pallas import tpu as pltpu
from jax.sharding import PartitionSpec as P

mixing = 0.25
F32 = jnp.float32
BF16 = jnp.bfloat16
MIB = 2**20
VMEM = pltpu.VMEM
RANK = 8


def vmem_specs(count):
    return [pl.BlockSpec(memory_space=VMEM)] * count


def hbm_specs(count):
    return [pl.BlockSpec(memory_space=pltpu.HBM)] * count


def in_vmem(*arrays):
    return [pltpu.with_memory_space_constraint(array, VMEM) for array in arrays]


def in_hbm(*arrays):
    return [pltpu.with_memory_space_constraint(array, pltpu.HBM) for array in arrays]


def cost(size, rows):
    return pl.CostEstimate(flops=2 * size * rows, bytes_accessed=4 * size, transcendentals=0)


def pieces(value):
    high = value.astype(BF16).astype(F32)
    rest = value - high
    middle = rest.astype(BF16).astype(F32)
    return high, middle, rest - middle


def stack_of(value):
    return jnp.concatenate(pieces(value), axis=0).astype(BF16)


def weight_dot(stacked, weights, contract):
    high = weights.astype(BF16)
    low = (weights - high.astype(F32)).astype(BF16)
    dims = (((1,), (contract,)), ((), ()))
    total = lax.dot_general(stacked, high, dims, preferred_element_type=F32)
    total = total + lax.dot_general(stacked, low, dims, preferred_element_type=F32)
    rows = stacked.shape[0] // 3
    return total[:rows] + total[rows : 2 * rows] + total[2 * rows :]


def family_of(tile, tiles):
    family, place, start = 0, tile, 0
    for count in tiles[:-1]:
        start += count
        family = family + jnp.where(tile >= start, 1, 0)
        place = jnp.where(tile >= start, tile - start, place)
    return family, place


def image_kernel(tiles, tile, block, in_flight, *refs):
    weights, factors = refs[:3], refs[3:6]
    images, held = refs[6:8]
    brought, stack_ref, sems, factor_sems = refs[8:11], refs[11], refs[12], refs[13]
    rows = held.shape[0]
    blocks = rows // block
    jobs = sum(tiles) * blocks

    def copy_of(family, place, job):
        start, wide = (job % blocks) * block, (job // blocks) * tile
        column = place * tile
        if not isinstance(job, int):
            start, wide = pl.multiple_of(start, block), pl.multiple_of(wide, tile)
            column = pl.multiple_of(column, tile)
        source, target = weights[family].at[:, pl.ds(column, tile)], held.at[:, pl.ds(wide, tile)]
        sem = sems.at[job % in_flight]

        def copy(first, count):
            span = pl.ds(start + first, count)
            return pltpu.make_async_copy(source.at[span], target.at[span], sem)

        return copy

    def start_copies(family, place, job):
        copy = copy_of(family, place, job)
        for part in range(4):
            copy(part * (block // 4), block // 4).start(priority=part % 2)

    for job in range(min(jobs, in_flight)):
        start_copies(0, job // blocks, job)
    factor_copies = [
        pltpu.make_async_copy(factors[family], brought[family], factor_sems.at[family])
        for family in range(3)
    ]
    for copy in factor_copies:
        copy.start()
    offset = 0
    for family in range(3):
        columns = tiles[family] * tile
        factor_copies[family].wait()
        stack_ref[:, pl.ds(offset, columns)] = stack_of(brought[family][...])
        offset += columns
    images[...] = jnp.zeros_like(images)

    def step(job, carry):
        copy_of(0, 0, job)(0, block).wait()
        following = job + in_flight
        later, place = family_of(following // blocks, tiles)
        for family in range(3):

            @pl.when((later == family) & (following < jobs))
            def _():
                start_copies(family, place, following)

        span = pl.ds(pl.multiple_of((job % blocks) * block, block), block)
        wide = pl.ds(pl.multiple_of((job // blocks) * tile, tile), tile)
        part = weight_dot(stack_ref[:, wide], held[span, wide], 1)
        family, _ = family_of(job // blocks, tiles)
        images[pl.ds(pl.multiple_of(RANK * family, RANK), RANK), span] += part
        return carry

    lax.fori_loop(0, jobs, step, 0)


def images_of(weights, factors, tiles, tile):
    rows = weights[0].shape[0]
    columns = sum(tiles) * tile
    block = min(rows, 512)
    in_flight = min(2, tiles[0] * (rows // block))
    return pl.pallas_call(
        functools.partial(image_kernel, tiles, tile, block, in_flight),
        out_shape=(jax.ShapeDtypeStruct((3 * RANK, rows), F32), VMEM((rows, columns), F32)),
        in_specs=hbm_specs(6),
        out_specs=tuple(vmem_specs(2)),
        scratch_shapes=[VMEM(factor.shape, F32) for factor in factors]
        + [
            VMEM((3 * RANK, columns), BF16),
            pltpu.SemaphoreType.DMA((in_flight,)),
            pltpu.SemaphoreType.DMA((3,)),
        ],
        compiler_params=pltpu.CompilerParams(vmem_limit_bytes=8 * MIB),
        cost_estimate=cost(rows * columns, RANK),
        name="images",
    )(*in_hbm(*weights, *factors))


def project_half(tiles, tile, part, stack_ref, held, out):
    half = sum(tiles) // 2

    def step(index, carry):
        index = part * half + index
        family, _ = family_of(index, tiles)
        wide = pl.ds(pl.multiple_of(index * tile, tile), tile)
        span = pl.ds(pl.multiple_of(128 + (index % half) * tile, 128), tile)
        out[:, span] = weight_dot(stack_ref[family], held[:, wide], 0)
        return carry

    lax.fori_loop(0, half, step, 0, unroll=3)


def send_kernel(sides, tiles, tile, here, after, before, held, leads, stack_ref, send):
    core = lax.rem(lax.axis_index("fsdp"), 2)
    images = here[...]
    right = images - after[...]
    left = before[...] - images
    rows = RANK * sides
    grams = []
    for family in range(3):
        mine = slice(RANK * family, RANK * family + RANK)
        lead = right[mine] if sides == 1 else jnp.concatenate([right[mine], left[mine]], axis=0)
        leads[pl.ds(rows * family, rows), :] = lead
        stack_ref[family] = stack_of(lead)
        grams.append(
            lax.dot_general(
                lead,
                lead,
                (((1,), (1,)), ((), ())),
                precision=lax.Precision.HIGHEST,
                preferred_element_type=F32,
            )
        )
    send[:, pl.ds(0, 128)] = jnp.concatenate(grams + [jnp.zeros((rows, 128 - 3 * rows), F32)], axis=1)
    project_half(tiles, tile, 1 - core, stack_ref, held, send)


def keep_kernel(tiles, tile, stack_ref, send, held, keep):
    core = lax.rem(lax.axis_index("fsdp"), 2)
    keep[:, pl.ds(0, 128)] = send[:, pl.ds(0, 128)]
    project_half(tiles, tile, core, stack_ref, held, keep)


def project(sides, tiles, tile, here, after, before, held):
    rows = RANK * sides
    width = held.shape[1] // 2 + 128
    params = pltpu.CompilerParams(vmem_limit_bytes=12 * MIB)
    estimate = cost(held.size // 2, 2 * RANK)
    leads, stack, send = pl.pallas_call(
        functools.partial(send_kernel, sides, tiles, tile),
        out_shape=(
            jax.ShapeDtypeStruct((3 * rows, here.shape[1]), F32),
            jax.ShapeDtypeStruct((3, 3 * rows, here.shape[1]), BF16),
            jax.ShapeDtypeStruct((rows, width), F32),
        ),
        in_specs=vmem_specs(4),
        out_specs=tuple(vmem_specs(3)),
        compiler_params=params,
        cost_estimate=estimate,
        name="project_send",
    )(here, after, before, *in_vmem(held))
    keep = pl.pallas_call(
        functools.partial(keep_kernel, tiles, tile),
        out_shape=jax.ShapeDtypeStruct((rows, width), F32),
        in_specs=vmem_specs(3),
        out_specs=vmem_specs(1)[0],
        compiler_params=params,
        cost_estimate=estimate,
        name="project_keep",
    )(stack, send, *in_vmem(held))
    return leads, keep, send


def inverse_cholesky(grams):
    shape = (RANK, RANK)
    row = lax.broadcasted_iota(jnp.int32, shape, 0)
    unit = (row == lax.broadcasted_iota(jnp.int32, shape, 1)).astype(F32)
    tables = [jnp.concatenate([gram, unit], axis=1) for gram in grams]
    below = lax.broadcasted_iota(jnp.int32, (RANK, 1), 0)
    for step in range(RANK):
        after = []
        for table in tables:
            pivot = table[step : step + 1, step : step + 1]
            scale = lax.rsqrt(pivot)
            scale = scale * (1.5 - 0.5 * pivot * scale * scale)
            lead = table[step : step + 1, :] * scale
            factor = table[:, step : step + 1] * scale
            lowered = table - factor * lead
            after.append(jnp.where(below < step, table, jnp.where(below == step, lead, lowered)))
        tables = after
    return [table[:, RANK:] for table in tables]


def apply_rows(matrix, values):
    total = matrix[:, 0:1] * values[0:1, :]
    for index in range(1, RANK):
        total = total + matrix[:, index : index + 1] * values[index : index + 1, :]
    return total


def normalise_kernel(sides, grams, leads, inverses, bases):
    rows = RANK * sides
    tables = []
    for family in range(3):
        for side in range(sides):
            span = slice(RANK * side, RANK * side + RANK)
            start = rows * family + RANK * side
            tables.append(grams[span, start : start + RANK])
    solved = inverse_cholesky(tables)
    for family in range(3):
        basis = []
        for side in range(sides):
            inverse = solved[sides * family + side]
            inverses[family, side] = inverse
            basis.append(apply_rows(inverse, leads[pl.ds(rows * family + RANK * side, RANK), :]))
        high, middle, low = pieces(jnp.concatenate(basis, axis=0) if sides > 1 else basis[0])
        bases[family] = jnp.concatenate([high, high, high, middle, middle, low], axis=0).astype(BF16)


def normalise(sides, grams, leads):
    rows = RANK * sides
    return pl.pallas_call(
        functools.partial(normalise_kernel, sides),
        out_shape=(
            jax.ShapeDtypeStruct((3, sides, RANK, RANK), F32),
            jax.ShapeDtypeStruct((3, 6 * rows, leads.shape[1]), BF16),
        ),
        in_specs=vmem_specs(2),
        out_specs=tuple(vmem_specs(2)),
        compiler_params=pltpu.CompilerParams(vmem_limit_bytes=4 * MIB),
        cost_estimate=pl.CostEstimate(flops=10**6, bytes_accessed=4 * MIB, transcendentals=48),
        name="normalise",
    )(grams, leads)


def update_kernel(sides, tiles, slots, inverses, bases, mine, other, held, *refs):
    mixed, following = refs[:3], refs[3:6]
    stage, coeff_ref, sems = refs[6:]
    core = lax.rem(lax.axis_index("fsdp"), 2)
    block, tile = stage.shape[1:]
    blocks = held.shape[0] // block
    half = sum(tiles) // 2
    factor = mixing * (2 // sides)

    def copy_of(family, place, job, slot):
        start = pl.multiple_of((job % blocks) * block, block)
        column = pl.multiple_of(place * tile, tile)
        target = mixed[family].at[0, pl.ds(start, block), pl.ds(column, tile)]
        return pltpu.make_async_copy(stage.at[slot], target, sems.at[slot])

    def change(job, carry):
        slot = job % slots
        index = job // blocks
        family, place = family_of(index, tiles)

        @pl.when(job % blocks == 0)
        def _():
            span = pl.ds(pl.multiple_of((index % half) * tile, tile), tile)
            chosen = jnp.where(core == index // half, mine[:, span], other[:, span])
            renewed = [
                apply_rows(inverses[family, side], chosen[RANK * side : RANK * side + RANK])
                for side in range(sides)
            ]
            for which in range(3):

                @pl.when(family == which)
                def _():
                    following[which][0, :, pl.ds(pl.multiple_of(place * tile, tile), tile)] = renewed[0]

            coeff = renewed[0] if sides == 1 else jnp.concatenate([renewed[0], -renewed[1]], axis=0)
            high, middle, low = pieces(coeff)
            coeff_ref[...] = jnp.concatenate([high, middle, low, high, middle, high], axis=0).astype(BF16)

        @pl.when(job >= slots)
        def _():
            copy_of(0, 0, 0, slot).wait()

        span = pl.ds(pl.multiple_of((job % blocks) * block, block), block)
        product = lax.dot_general(
            bases[family, :, span],
            coeff_ref[...],
            (((0,), (0,)), ((), ())),
            preferred_element_type=F32,
        )
        stage[slot] = held[span, pl.ds(pl.multiple_of(index * tile, tile), tile)] - factor * product
        for which in range(3):

            @pl.when(family == which)
            def _():
                copy_of(which, place, job, slot).start()

        return carry

    jobs = blocks * sum(tiles)
    lax.fori_loop(0, jobs, change, 0)
    for slot in range(min(slots, jobs)):
        copy_of(0, 0, 0, slot).wait()


def update(sides, tiles, tile, inverses, bases, mine, other, held):
    rows = held.shape[0]
    slots = 3
    return pl.pallas_call(
        functools.partial(update_kernel, sides, tiles, slots),
        out_shape=tuple(pltpu.HBM((1, rows, count * tile), F32) for count in tiles)
        + tuple(jax.ShapeDtypeStruct((1, RANK, count * tile), F32) for count in tiles),
        in_specs=vmem_specs(5),
        out_specs=tuple(hbm_specs(3) + vmem_specs(3)),
        scratch_shapes=[
            VMEM((slots, min(512, rows), tile), F32),
            VMEM((6 * RANK * sides, tile), BF16),
            pltpu.SemaphoreType.DMA((slots,)),
        ],
        compiler_params=pltpu.CompilerParams(vmem_limit_bytes=12 * MIB),
        cost_estimate=cost(held.size, 2 * RANK),
        name="update",
    )(inverses, bases, mine, other, *in_vmem(held))


def moved(value, axis, target):
    count = lax.axis_size(axis)
    return lax.ppermute(value, axis, [(source, target(source, count)) for source in range(count)])


def along(value, distance):
    return moved(value, "rep", lambda source, count: (source + distance) % count)


def swapped(value, bit):
    return moved(value, "fsdp", lambda source, count: source ^ bit)


def summed(value):
    bit = 2
    while bit < lax.axis_size("fsdp"):
        value = value + swapped(value, bit)
        bit *= 2
    return value


def differences(distance, sides, values):
    right = values[:RANK]
    if sides == 1:
        return right + along(right, distance)
    left = values[RANK:]
    return jnp.concatenate([right - along(left, -distance), along(right, distance) - left], axis=0)


def one_round(tiles, tile, distance, images, held):
    sides = 1 if 2 * distance == lax.axis_size("rep") else 2
    after = along(images, -distance)
    before = after if sides == 1 else along(images, distance)
    leads, keep, send = project(sides, tiles, tile, images, after, before, held)
    total = keep + swapped(send, 1)
    parts = differences(distance, sides, total[:, 128:])
    parts = summed(jnp.concatenate([total[:, :128], parts], axis=1))
    mine = parts[:, 128:]
    other = swapped(mine, 1)
    inverses, bases = normalise(sides, parts[:, :128], leads)
    return update(sides, tiles, tile, inverses, bases, mine, other, held)


def per_device(query_weights, key_weights, value_weights, query_factor, key_factor, value_factor, step_index):
    weights = (query_weights[0], key_weights[0], value_weights[0])
    levels = lax.axis_size("rep").bit_length() - 1
    tile = min(1024, *[matrix.shape[1] for matrix in weights])
    tiles = tuple(matrix.shape[1] // tile for matrix in weights)
    images, held = images_of(weights, (query_factor, key_factor, value_factor), tiles, tile)
    branches = [functools.partial(one_round, tiles, tile, 1 << level) for level in range(levels)]
    return lax.switch(step_index[0] % levels, branches, images, held)


def solution(mesh):
    split = P("rep", "fsdp", None)
    return jax.shard_map(
        per_device,
        mesh=mesh,
        in_specs=(split, split, split, P(), P(), P(), P()),
        out_specs=(split, split, split) + (P("rep", None, None),) * 3,
        check_vma=False,
    )
```

```python
import functools

import jax
import jax.numpy as jnp
from jax import lax
from jax.experimental import pallas as pl
from jax.experimental.pallas import tpu as pltpu
from jax.sharding import PartitionSpec as P

mixing = 0.25
F32 = jnp.float32
BF16 = jnp.bfloat16
MIB = 2**20
VMEM = pltpu.VMEM
RANK = 8


def vmem_specs(count):
    return [pl.BlockSpec(memory_space=VMEM)] * count


def hbm_specs(count):
    return [pl.BlockSpec(memory_space=pltpu.HBM)] * count


def in_vmem(*arrays):
    return [pltpu.with_memory_space_constraint(array, VMEM) for array in arrays]


def in_hbm(*arrays):
    return [pltpu.with_memory_space_constraint(array, pltpu.HBM) for array in arrays]


def cost(size, rows):
    return pl.CostEstimate(flops=2 * size * rows, bytes_accessed=4 * size, transcendentals=0)


def pieces(value):
    high = value.astype(BF16).astype(F32)
    rest = value - high
    middle = rest.astype(BF16).astype(F32)
    return high, middle, rest - middle


def stack_of(value):
    return jnp.concatenate(pieces(value), axis=0).astype(BF16)


def weight_dot(stacked, weights, contract):
    high = weights.astype(BF16)
    low = (weights - high.astype(F32)).astype(BF16)
    dims = (((1,), (contract,)), ((), ()))
    total = lax.dot_general(stacked, high, dims, preferred_element_type=F32)
    total = total + lax.dot_general(stacked, low, dims, preferred_element_type=F32)
    rows = stacked.shape[0] // 3
    return total[:rows] + total[rows : 2 * rows] + total[2 * rows :]


def family_of(tile, tiles):
    family, place, start = 0, tile, 0
    for count in tiles[:-1]:
        start += count
        family = family + jnp.where(tile >= start, 1, 0)
        place = jnp.where(tile >= start, tile - start, place)
    return family, place


def image_kernel(tiles, tile, block, in_flight, *refs):
    weights, factors = refs[:3], refs[3:6]
    images, held = refs[6:8]
    brought, stack_ref, sems, factor_sems = refs[8:11], refs[11], refs[12], refs[13]
    rows = held.shape[0]
    blocks = rows // block
    jobs = sum(tiles) * blocks

    def copy_of(family, place, job):
        start, wide = (job % blocks) * block, (job // blocks) * tile
        column = place * tile
        if not isinstance(job, int):
            start, wide = pl.multiple_of(start, block), pl.multiple_of(wide, tile)
            column = pl.multiple_of(column, tile)
        source, target = weights[family].at[:, pl.ds(column, tile)], held.at[:, pl.ds(wide, tile)]
        sem = sems.at[job % in_flight]

        def copy(first, count):
            span = pl.ds(start + first, count)
            return pltpu.make_async_copy(source.at[span], target.at[span], sem)

        return copy

    def start_copies(family, place, job):
        copy = copy_of(family, place, job)
        for part in range(4):
            copy(part * (block // 4), block // 4).start(priority=part % 2)

    for job in range(min(jobs, in_flight)):
        start_copies(0, job // blocks, job)
    factor_copies = [
        pltpu.make_async_copy(factors[family], brought[family], factor_sems.at[family])
        for family in range(3)
    ]
    for copy in factor_copies:
        copy.start()
    offset = 0
    for family in range(3):
        columns = tiles[family] * tile
        factor_copies[family].wait()
        stack_ref[:, pl.ds(offset, columns)] = stack_of(brought[family][...])
        offset += columns
    images[...] = jnp.zeros_like(images)

    def step(job, carry):
        copy_of(0, 0, job)(0, block).wait()
        following = job + in_flight
        later, place = family_of(following // blocks, tiles)
        for family in range(3):

            @pl.when((later == family) & (following < jobs))
            def _():
                start_copies(family, place, following)

        span = pl.ds(pl.multiple_of((job % blocks) * block, block), block)
        wide = pl.ds(pl.multiple_of((job // blocks) * tile, tile), tile)
        part = weight_dot(stack_ref[:, wide], held[span, wide], 1)
        family, _ = family_of(job // blocks, tiles)
        images[pl.ds(pl.multiple_of(RANK * family, RANK), RANK), span] += part
        return carry

    lax.fori_loop(0, jobs, step, 0)


def images_of(weights, factors, tiles, tile):
    rows = weights[0].shape[0]
    columns = sum(tiles) * tile
    block = min(rows, 512)
    in_flight = min(2, tiles[0] * (rows // block))
    return pl.pallas_call(
        functools.partial(image_kernel, tiles, tile, block, in_flight),
        out_shape=(jax.ShapeDtypeStruct((3 * RANK, rows), F32), VMEM((rows, columns), F32)),
        in_specs=hbm_specs(6),
        out_specs=tuple(vmem_specs(2)),
        scratch_shapes=[VMEM(factor.shape, F32) for factor in factors]
        + [
            VMEM((3 * RANK, columns), BF16),
            pltpu.SemaphoreType.DMA((in_flight,)),
            pltpu.SemaphoreType.DMA((3,)),
        ],
        compiler_params=pltpu.CompilerParams(vmem_limit_bytes=8 * MIB),
        cost_estimate=cost(rows * columns, RANK),
        name="images",
    )(*in_hbm(*weights, *factors))


def project_half(tiles, tile, part, stack_ref, held, out):
    half = sum(tiles) // 2

    def step(index, carry):
        index = part * half + index
        family, _ = family_of(index, tiles)
        wide = pl.ds(pl.multiple_of(index * tile, tile), tile)
        span = pl.ds(pl.multiple_of(128 + (index % half) * tile, 128), tile)
        out[:, span] = weight_dot(stack_ref[family], held[:, wide], 0)
        return carry

    lax.fori_loop(0, half, step, 0, unroll=3)


def send_kernel(sides, tiles, tile, here, after, before, held, leads, stack_ref, send):
    core = lax.rem(lax.axis_index("fsdp"), 2)
    images = here[...]
    right = images - after[...]
    left = before[...] - images
    rows = RANK * sides
    grams = []
    for family in range(3):
        mine = slice(RANK * family, RANK * family + RANK)
        lead = right[mine] if sides == 1 else jnp.concatenate([right[mine], left[mine]], axis=0)
        leads[pl.ds(rows * family, rows), :] = lead
        stack_ref[family] = stack_of(lead)
        grams.append(
            lax.dot_general(
                lead,
                lead,
                (((1,), (1,)), ((), ())),
                precision=lax.Precision.HIGHEST,
                preferred_element_type=F32,
            )
        )
    send[:, pl.ds(0, 128)] = jnp.concatenate(grams + [jnp.zeros((rows, 128 - 3 * rows), F32)], axis=1)
    project_half(tiles, tile, 1 - core, stack_ref, held, send)


def keep_kernel(tiles, tile, stack_ref, send, held, keep):
    core = lax.rem(lax.axis_index("fsdp"), 2)
    keep[:, pl.ds(0, 128)] = send[:, pl.ds(0, 128)]
    project_half(tiles, tile, core, stack_ref, held, keep)


def project(sides, tiles, tile, here, after, before, held):
    rows = RANK * sides
    width = held.shape[1] // 2 + 128
    params = pltpu.CompilerParams(vmem_limit_bytes=12 * MIB)
    estimate = cost(held.size // 2, 2 * RANK)
    leads, stack, send = pl.pallas_call(
        functools.partial(send_kernel, sides, tiles, tile),
        out_shape=(
            jax.ShapeDtypeStruct((3 * rows, here.shape[1]), F32),
            jax.ShapeDtypeStruct((3, 3 * rows, here.shape[1]), BF16),
            jax.ShapeDtypeStruct((rows, width), F32),
        ),
        in_specs=vmem_specs(4),
        out_specs=tuple(vmem_specs(3)),
        compiler_params=params,
        cost_estimate=estimate,
        name="project_send",
    )(here, after, before, *in_vmem(held))
    keep = pl.pallas_call(
        functools.partial(keep_kernel, tiles, tile),
        out_shape=jax.ShapeDtypeStruct((rows, width), F32),
        in_specs=vmem_specs(3),
        out_specs=vmem_specs(1)[0],
        compiler_params=params,
        cost_estimate=estimate,
        name="project_keep",
    )(stack, send, *in_vmem(held))
    return leads, keep, send


def inverse_cholesky(grams):
    shape = (RANK, RANK)
    row = lax.broadcasted_iota(jnp.int32, shape, 0)
    unit = (row == lax.broadcasted_iota(jnp.int32, shape, 1)).astype(F32)
    tables = [jnp.concatenate([gram, unit], axis=1) for gram in grams]
    below = lax.broadcasted_iota(jnp.int32, (RANK, 1), 0)
    for step in range(RANK):
        after = []
        for table in tables:
            pivot = table[step : step + 1, step : step + 1]
            scale = lax.rsqrt(pivot)
            scale = scale * (1.5 - 0.5 * pivot * scale * scale)
            lead = table[step : step + 1, :] * scale
            factor = table[:, step : step + 1] * scale
            lowered = table - factor * lead
            after.append(jnp.where(below < step, table, jnp.where(below == step, lead, lowered)))
        tables = after
    return [table[:, RANK:] for table in tables]


def apply_rows(matrix, values):
    total = matrix[:, 0:1] * values[0:1, :]
    for index in range(1, RANK):
        total = total + matrix[:, index : index + 1] * values[index : index + 1, :]
    return total


def normalise_kernel(sides, grams, leads, inverses, bases):
    rows = RANK * sides
    tables = []
    for family in range(3):
        for side in range(sides):
            span = slice(RANK * side, RANK * side + RANK)
            start = rows * family + RANK * side
            tables.append(grams[span, start : start + RANK])
    solved = inverse_cholesky(tables)
    for family in range(3):
        basis = []
        for side in range(sides):
            inverse = solved[sides * family + side]
            inverses[family, side] = inverse
            basis.append(apply_rows(inverse, leads[pl.ds(rows * family + RANK * side, RANK), :]))
        high, middle, low = pieces(jnp.concatenate(basis, axis=0) if sides > 1 else basis[0])
        bases[family] = jnp.concatenate([high, high, high, middle, middle, low], axis=0).astype(BF16)


def normalise(sides, grams, leads):
    rows = RANK * sides
    return pl.pallas_call(
        functools.partial(normalise_kernel, sides),
        out_shape=(
            jax.ShapeDtypeStruct((3, sides, RANK, RANK), F32),
            jax.ShapeDtypeStruct((3, 6 * rows, leads.shape[1]), BF16),
        ),
        in_specs=vmem_specs(2),
        out_specs=tuple(vmem_specs(2)),
        compiler_params=pltpu.CompilerParams(vmem_limit_bytes=4 * MIB),
        cost_estimate=pl.CostEstimate(flops=10**6, bytes_accessed=4 * MIB, transcendentals=48),
        name="normalise",
    )(grams, leads)


def update_kernel(sides, tiles, slots, inverses, bases, mine, other, held, *refs):
    mixed, following = refs[:3], refs[3:6]
    stage, coeff_ref, sems = refs[6:]
    core = lax.rem(lax.axis_index("fsdp"), 2)
    block, tile = stage.shape[1:]
    blocks = held.shape[0] // block
    half = sum(tiles) // 2
    factor = mixing * (2 // sides)

    def copy_of(family, place, job, slot):
        start = pl.multiple_of((job % blocks) * block, block)
        column = pl.multiple_of(place * tile, tile)
        target = mixed[family].at[0, pl.ds(start, block), pl.ds(column, tile)]
        return pltpu.make_async_copy(stage.at[slot], target, sems.at[slot])

    def change(job, carry):
        slot = job % slots
        index = job // blocks
        family, place = family_of(index, tiles)

        @pl.when(job % blocks == 0)
        def _():
            span = pl.ds(pl.multiple_of((index % half) * tile, tile), tile)
            chosen = jnp.where(core == index // half, mine[:, span], other[:, span])
            renewed = [
                apply_rows(inverses[family, side], chosen[RANK * side : RANK * side + RANK])
                for side in range(sides)
            ]
            for which in range(3):

                @pl.when(family == which)
                def _():
                    following[which][0, :, pl.ds(pl.multiple_of(place * tile, tile), tile)] = renewed[0]

            coeff = renewed[0] if sides == 1 else jnp.concatenate([renewed[0], -renewed[1]], axis=0)
            high, middle, low = pieces(coeff)
            coeff_ref[...] = jnp.concatenate([high, middle, low, high, middle, high], axis=0).astype(BF16)

        @pl.when(job >= slots)
        def _():
            copy_of(0, 0, 0, slot).wait()

        span = pl.ds(pl.multiple_of((job % blocks) * block, block), block)
        product = lax.dot_general(
            bases[family, :, span],
            coeff_ref[...],
            (((0,), (0,)), ((), ())),
            preferred_element_type=F32,
        )
        stage[slot] = held[span, pl.ds(pl.multiple_of(index * tile, tile), tile)] - factor * product
        for which in range(3):

            @pl.when(family == which)
            def _():
                copy_of(which, place, job, slot).start()

        return carry

    jobs = blocks * sum(tiles)
    lax.fori_loop(0, jobs, change, 0)
    for slot in range(min(slots, jobs)):
        copy_of(0, 0, 0, slot).wait()


def update(sides, tiles, tile, inverses, bases, mine, other, held):
    rows = held.shape[0]
    slots = 3
    return pl.pallas_call(
        functools.partial(update_kernel, sides, tiles, slots),
        out_shape=tuple(pltpu.HBM((1, rows, count * tile), F32) for count in tiles)
        + tuple(jax.ShapeDtypeStruct((1, RANK, count * tile), F32) for count in tiles),
        in_specs=vmem_specs(5),
        out_specs=tuple(hbm_specs(3) + vmem_specs(3)),
        scratch_shapes=[
            VMEM((slots, min(512, rows), tile), F32),
            VMEM((6 * RANK * sides, tile), BF16),
            pltpu.SemaphoreType.DMA((slots,)),
        ],
        compiler_params=pltpu.CompilerParams(vmem_limit_bytes=12 * MIB),
        cost_estimate=cost(held.size, 2 * RANK),
        name="update",
    )(inverses, bases, mine, other, *in_vmem(held))


def moved(value, axis, target):
    count = lax.axis_size(axis)
    return lax.ppermute(value, axis, [(source, target(source, count)) for source in range(count)])


def along(value, distance):
    return moved(value, "rep", lambda source, count: (source + distance) % count)


def swapped(value, bit):
    return moved(value, "fsdp", lambda source, count: source ^ bit)


def across(value, distance):
    replicas, count = lax.axis_size("rep"), lax.axis_size("fsdp")
    pairs = [
        (replica * count + place, (replica + distance) % replicas * count + (place ^ 2))
        for replica in range(replicas)
        for place in range(count)
    ]
    return lax.ppermute(value, ("rep", "fsdp"), pairs)


def summed(value, bit):
    while bit < lax.axis_size("fsdp"):
        value = value + swapped(value, bit)
        bit *= 2
    return value


def differences(distance, sides, total):
    if sides == 1:
        right = total[:, 128:]
        return summed(jnp.concatenate([total[:, :128], right + along(right, distance)], axis=1), 2)
    total = summed(total, 4)
    right, left = total[:RANK, 128:], total[RANK:, 128:]
    ahead, behind = along(left, -distance), along(right, distance)
    if lax.axis_size("fsdp") > 2:
        ahead, behind = ahead + across(left, -distance), behind + across(right, distance)
        total = total + swapped(total, 2)
    parts = jnp.concatenate([total[:RANK, 128:] - ahead, behind - total[RANK:, 128:]], axis=0)
    return jnp.concatenate([total[:, :128], parts], axis=1)


def one_round(tiles, tile, distance, images, held):
    sides = 1 if 2 * distance == lax.axis_size("rep") else 2
    after = along(images, -distance)
    before = after if sides == 1 else along(images, distance)
    leads, keep, send = project(sides, tiles, tile, images, after, before, held)
    total = keep + swapped(send, 1)
    parts = differences(distance, sides, total)
    mine = parts[:, 128:]
    other = swapped(mine, 1)
    inverses, bases = normalise(sides, parts[:, :128], leads)
    return update(sides, tiles, tile, inverses, bases, mine, other, held)


def per_device(query_weights, key_weights, value_weights, query_factor, key_factor, value_factor, step_index):
    weights = (query_weights[0], key_weights[0], value_weights[0])
    levels = lax.axis_size("rep").bit_length() - 1
    tile = min(1024, *[matrix.shape[1] for matrix in weights])
    tiles = tuple(matrix.shape[1] // tile for matrix in weights)
    images, held = images_of(weights, (query_factor, key_factor, value_factor), tiles, tile)
    branches = [functools.partial(one_round, tiles, tile, 1 << level) for level in range(levels)]
    return lax.switch(step_index[0] % levels, branches, images, held)


def solution(mesh):
    split = P("rep", "fsdp", None)
    return jax.shard_map(
        per_device,
        mesh=mesh,
        in_specs=(split, split, split, P(), P(), P(), P()),
        out_specs=(split, split, split) + (P("rep", None, None),) * 3,
        check_vma=False,
    )
```

```python
import functools

import jax
import jax.numpy as jnp
from jax import lax
from jax.experimental import pallas as pl
from jax.experimental.pallas import tpu as pltpu
from jax.sharding import PartitionSpec as P

mixing = 0.25
F32 = jnp.float32
BF16 = jnp.bfloat16
MIB = 2**20
VMEM = pltpu.VMEM
RANK = 8


def vmem_specs(count):
    return [pl.BlockSpec(memory_space=VMEM)] * count


def hbm_specs(count):
    return [pl.BlockSpec(memory_space=pltpu.HBM)] * count


def in_vmem(*arrays):
    return [pltpu.with_memory_space_constraint(array, VMEM) for array in arrays]


def in_hbm(*arrays):
    return [pltpu.with_memory_space_constraint(array, pltpu.HBM) for array in arrays]


def cost(size, rows):
    return pl.CostEstimate(flops=2 * size * rows, bytes_accessed=4 * size, transcendentals=0)


def pieces(value):
    high = value.astype(BF16).astype(F32)
    rest = value - high
    middle = rest.astype(BF16).astype(F32)
    return high, middle, rest - middle


def stack_of(value):
    return jnp.concatenate(pieces(value), axis=0).astype(BF16)


def weight_dot(stacked, weights, contract):
    high = weights.astype(BF16)
    low = (weights - high.astype(F32)).astype(BF16)
    dims = (((1,), (contract,)), ((), ()))
    total = lax.dot_general(stacked, high, dims, preferred_element_type=F32)
    total = total + lax.dot_general(stacked, low, dims, preferred_element_type=F32)
    rows = stacked.shape[0] // 3
    return total[:rows] + total[rows : 2 * rows] + total[2 * rows :]


def family_of(tile, tiles):
    family, place, start = 0, tile, 0
    for count in tiles[:-1]:
        start += count
        family = family + jnp.where(tile >= start, 1, 0)
        place = jnp.where(tile >= start, tile - start, place)
    return family, place


def image_kernel(tiles, tile, block, in_flight, *refs):
    weights, factors = refs[:3], refs[3:6]
    images, held = refs[6:8]
    brought, stack_ref, sems, factor_sems = refs[8:11], refs[11], refs[12], refs[13]
    rows = held.shape[0]
    blocks = rows // block
    jobs = sum(tiles) * blocks

    def copy_of(family, place, job):
        start, wide = (job % blocks) * block, (job // blocks) * tile
        column = place * tile
        if not isinstance(job, int):
            start, wide = pl.multiple_of(start, block), pl.multiple_of(wide, tile)
            column = pl.multiple_of(column, tile)
        source, target = weights[family].at[:, pl.ds(column, tile)], held.at[:, pl.ds(wide, tile)]
        sem = sems.at[job % in_flight]

        def copy(first, count):
            span = pl.ds(start + first, count)
            return pltpu.make_async_copy(source.at[span], target.at[span], sem)

        return copy

    def start_copies(family, place, job):
        copy = copy_of(family, place, job)
        for part in range(4):
            copy(part * (block // 4), block // 4).start(priority=part % 2)

    for job in range(min(jobs, in_flight)):
        start_copies(0, job // blocks, job)
    factor_copies = [
        pltpu.make_async_copy(factors[family], brought[family], factor_sems.at[family])
        for family in range(3)
    ]
    for copy in factor_copies:
        copy.start()
    offset = 0
    for family in range(3):
        columns = tiles[family] * tile
        factor_copies[family].wait()
        stack_ref[:, pl.ds(offset, columns)] = stack_of(brought[family][...])
        offset += columns
    images[...] = jnp.zeros_like(images)

    def step(job, carry):
        copy_of(0, 0, job)(0, block).wait()
        following = job + in_flight
        later, place = family_of(following // blocks, tiles)
        for family in range(3):

            @pl.when((later == family) & (following < jobs))
            def _():
                start_copies(family, place, following)

        span = pl.ds(pl.multiple_of((job % blocks) * block, block), block)
        wide = pl.ds(pl.multiple_of((job // blocks) * tile, tile), tile)
        part = weight_dot(stack_ref[:, wide], held[span, wide], 1)
        family, _ = family_of(job // blocks, tiles)
        images[pl.ds(pl.multiple_of(RANK * family, RANK), RANK), span] += part
        return carry

    lax.fori_loop(0, jobs, step, 0)


def images_of(weights, factors, tiles, tile):
    rows = weights[0].shape[0]
    columns = sum(tiles) * tile
    block = min(rows, 512)
    in_flight = min(2, tiles[0] * (rows // block))
    return pl.pallas_call(
        functools.partial(image_kernel, tiles, tile, block, in_flight),
        out_shape=(jax.ShapeDtypeStruct((3 * RANK, rows), F32), VMEM((rows, columns), F32)),
        in_specs=hbm_specs(6),
        out_specs=tuple(vmem_specs(2)),
        scratch_shapes=[VMEM(factor.shape, F32) for factor in factors]
        + [
            VMEM((3 * RANK, columns), BF16),
            pltpu.SemaphoreType.DMA((in_flight,)),
            pltpu.SemaphoreType.DMA((3,)),
        ],
        compiler_params=pltpu.CompilerParams(vmem_limit_bytes=8 * MIB),
        cost_estimate=cost(rows * columns, RANK),
        name="images",
    )(*in_hbm(*weights, *factors))


def project_half(tiles, tile, part, stack_ref, held, out):
    half = sum(tiles) // 2

    def step(index, carry):
        index = part * half + index
        family, _ = family_of(index, tiles)
        wide = pl.ds(pl.multiple_of(index * tile, tile), tile)
        span = pl.ds(pl.multiple_of(128 + (index % half) * tile, 128), tile)
        out[:, span] = weight_dot(stack_ref[family], held[:, wide], 0)
        return carry

    lax.fori_loop(0, half, step, 0, unroll=3)


def send_kernel(sides, tiles, tile, here, after, before, held, leads, stack_ref, send):
    core = lax.rem(lax.axis_index("fsdp"), 2)
    images = here[...]
    right = images - after[...]
    left = before[...] - images
    rows = RANK * sides
    grams = []
    for family in range(3):
        mine = slice(RANK * family, RANK * family + RANK)
        lead = right[mine] if sides == 1 else jnp.concatenate([right[mine], left[mine]], axis=0)
        leads[pl.ds(rows * family, rows), :] = lead
        stack_ref[family] = stack_of(lead)
        grams.append(
            lax.dot_general(
                lead,
                lead,
                (((1,), (1,)), ((), ())),
                precision=lax.Precision.HIGHEST,
                preferred_element_type=F32,
            )
        )
    send[:, pl.ds(0, 128)] = jnp.concatenate(grams + [jnp.zeros((rows, 128 - 3 * rows), F32)], axis=1)
    project_half(tiles, tile, 1 - core, stack_ref, held, send)


def keep_kernel(tiles, tile, stack_ref, send, held, keep):
    core = lax.rem(lax.axis_index("fsdp"), 2)
    keep[:, pl.ds(0, 128)] = send[:, pl.ds(0, 128)]
    project_half(tiles, tile, core, stack_ref, held, keep)


def project(sides, tiles, tile, here, after, before, held):
    rows = RANK * sides
    width = held.shape[1] // 2 + 128
    params = pltpu.CompilerParams(vmem_limit_bytes=12 * MIB)
    estimate = cost(held.size // 2, 2 * RANK)
    leads, stack, send = pl.pallas_call(
        functools.partial(send_kernel, sides, tiles, tile),
        out_shape=(
            jax.ShapeDtypeStruct((3 * rows, here.shape[1]), F32),
            jax.ShapeDtypeStruct((3, 3 * rows, here.shape[1]), BF16),
            jax.ShapeDtypeStruct((rows, width), F32),
        ),
        in_specs=vmem_specs(4),
        out_specs=tuple(vmem_specs(3)),
        compiler_params=params,
        cost_estimate=estimate,
        name="project_send",
    )(here, after, before, *in_vmem(held))
    keep = pl.pallas_call(
        functools.partial(keep_kernel, tiles, tile),
        out_shape=jax.ShapeDtypeStruct((rows, width), F32),
        in_specs=vmem_specs(3),
        out_specs=vmem_specs(1)[0],
        compiler_params=params,
        cost_estimate=estimate,
        name="project_keep",
    )(stack, send, *in_vmem(held))
    return leads, keep, send


def inverse_cholesky(grams):
    shape = (RANK, RANK)
    row = lax.broadcasted_iota(jnp.int32, shape, 0)
    unit = (row == lax.broadcasted_iota(jnp.int32, shape, 1)).astype(F32)
    tables = [jnp.concatenate([gram, unit], axis=1) for gram in grams]
    below = lax.broadcasted_iota(jnp.int32, (RANK, 1), 0)
    for step in range(RANK):
        after = []
        for table in tables:
            pivot = table[step : step + 1, step : step + 1]
            scale = lax.rsqrt(pivot)
            scale = scale * (1.5 - 0.5 * pivot * scale * scale)
            lead = table[step : step + 1, :] * scale
            factor = table[:, step : step + 1] * scale
            lowered = table - factor * lead
            after.append(jnp.where(below < step, table, jnp.where(below == step, lead, lowered)))
        tables = after
    return [table[:, RANK:] for table in tables]


def apply_rows(matrix, values):
    total = matrix[:, 0:1] * values[0:1, :]
    for index in range(1, RANK):
        total = total + matrix[:, index : index + 1] * values[index : index + 1, :]
    return total


def normalise_kernel(sides, grams, leads, inverses, bases):
    rows = RANK * sides
    tables = []
    for family in range(3):
        for side in range(sides):
            span = slice(RANK * side, RANK * side + RANK)
            start = rows * family + RANK * side
            tables.append(grams[span, start : start + RANK])
    solved = inverse_cholesky(tables)
    for family in range(3):
        basis = []
        for side in range(sides):
            inverse = solved[sides * family + side]
            inverses[family, side] = inverse
            basis.append(apply_rows(inverse, leads[pl.ds(rows * family + RANK * side, RANK), :]))
        high, middle, low = pieces(jnp.concatenate(basis, axis=0) if sides > 1 else basis[0])
        stack = jnp.concatenate([high, high, high, middle, middle, low], axis=0)
        spare = jnp.zeros((128 - stack.shape[0], stack.shape[1]), F32)
        bases[family] = jnp.concatenate([stack, spare], axis=0).T.astype(BF16)


def normalise(sides, grams, leads):
    rows = RANK * sides
    return pl.pallas_call(
        functools.partial(normalise_kernel, sides),
        out_shape=(
            jax.ShapeDtypeStruct((3, sides, RANK, RANK), F32),
            jax.ShapeDtypeStruct((3, leads.shape[1], 128), BF16),
        ),
        in_specs=vmem_specs(2),
        out_specs=tuple(vmem_specs(2)),
        compiler_params=pltpu.CompilerParams(vmem_limit_bytes=4 * MIB),
        cost_estimate=pl.CostEstimate(flops=10**6, bytes_accessed=4 * MIB, transcendentals=48),
        name="normalise",
    )(grams, leads)


def update_kernel(sides, tiles, slots, inverses, bases, mine, other, held, *refs):
    mixed, following = refs[:3], refs[3:6]
    stage, coeff_ref, renewed_ref, sems, small_sems = refs[6:]
    core = lax.rem(lax.axis_index("fsdp"), 2)
    block, tile = stage.shape[1:]
    blocks = held.shape[0] // block
    half = sum(tiles) // 2
    factor = mixing * (2 // sides)

    def copy_of(family, place, job, slot):
        start = pl.multiple_of((job % blocks) * block, block)
        column = pl.multiple_of(place * tile, tile)
        target = mixed[family].at[0, pl.ds(start, block), pl.ds(column, tile)]
        return pltpu.make_async_copy(stage.at[slot], target, sems.at[slot])

    def small_copy(family, place, index):
        wide = pl.ds(pl.multiple_of(place * tile, tile), tile)
        target = following[family].at[0, :, wide]
        return pltpu.make_async_copy(renewed_ref.at[index], target, small_sems.at[index])

    def change(job, carry):
        slot = job % slots
        index = job // blocks
        family, place = family_of(index, tiles)

        @pl.when(job % blocks == 0)
        def _():
            span = pl.ds(pl.multiple_of((index % half) * tile, tile), tile)
            chosen = jnp.where(core == index // half, mine[:, span], other[:, span])
            renewed = [
                apply_rows(inverses[family, side], chosen[RANK * side : RANK * side + RANK])
                for side in range(sides)
            ]
            renewed_ref[index] = renewed[0]
            for which in range(3):

                @pl.when(family == which)
                def _():
                    small_copy(which, place, index).start()

            coeff = renewed[0] if sides == 1 else jnp.concatenate([renewed[0], -renewed[1]], axis=0)
            high, middle, low = pieces(coeff)
            spare = jnp.zeros((128 - 6 * coeff.shape[0], tile), F32)
            stack = jnp.concatenate([high, middle, low, high, middle, high, spare], axis=0)
            coeff_ref[...] = stack.astype(BF16)

        @pl.when(job >= slots)
        def _():
            copy_of(0, 0, 0, slot).wait()

        span = pl.ds(pl.multiple_of((job % blocks) * block, block), block)
        product = jnp.dot(bases[family, span, :], coeff_ref[...], preferred_element_type=F32)
        stage[slot] = held[span, pl.ds(pl.multiple_of(index * tile, tile), tile)] - factor * product
        for which in range(3):

            @pl.when(family == which)
            def _():
                copy_of(which, place, job, slot).start()

        return carry

    jobs = blocks * sum(tiles)
    lax.fori_loop(0, jobs, change, 0)
    for slot in range(min(slots, jobs)):
        copy_of(0, 0, 0, slot).wait()
    for index in range(sum(tiles)):
        small_copy(0, 0, index).wait()


def update(sides, tiles, tile, inverses, bases, mine, other, held):
    rows = held.shape[0]
    slots = 3
    return pl.pallas_call(
        functools.partial(update_kernel, sides, tiles, slots),
        out_shape=tuple(pltpu.HBM((1, rows, count * tile), F32) for count in tiles)
        + tuple(pltpu.HBM((1, RANK, count * tile), F32) for count in tiles),
        in_specs=vmem_specs(5),
        out_specs=tuple(hbm_specs(6)),
        scratch_shapes=[
            VMEM((slots, min(512, rows), tile), F32),
            VMEM((128, tile), BF16),
            VMEM((sum(tiles), RANK, tile), F32),
            pltpu.SemaphoreType.DMA((slots,)),
            pltpu.SemaphoreType.DMA((sum(tiles),)),
        ],
        compiler_params=pltpu.CompilerParams(vmem_limit_bytes=12 * MIB),
        cost_estimate=cost(held.size, 2 * RANK),
        name="update",
    )(inverses, bases, mine, other, *in_vmem(held))


def moved(value, axis, target):
    count = lax.axis_size(axis)
    return lax.ppermute(value, axis, [(source, target(source, count)) for source in range(count)])


def along(value, distance):
    return moved(value, "rep", lambda source, count: (source + distance) % count)


def swapped(value, bit):
    return moved(value, "fsdp", lambda source, count: source ^ bit)


def across(value, distance):
    replicas, count = lax.axis_size("rep"), lax.axis_size("fsdp")
    pairs = [
        (replica * count + place, (replica + distance) % replicas * count + (place ^ 2))
        for replica in range(replicas)
        for place in range(count)
    ]
    return lax.ppermute(value, ("rep", "fsdp"), pairs)


def summed(value, bit):
    while bit < lax.axis_size("fsdp"):
        value = value + swapped(value, bit)
        bit *= 2
    return value


def differences(distance, sides, total):
    if sides == 1:
        right = total[:, 128:]
        return summed(jnp.concatenate([total[:, :128], right + along(right, distance)], axis=1), 2)
    total = summed(total, 4)
    right, left = total[:RANK, 128:], total[RANK:, 128:]
    ahead, behind = along(left, -distance), along(right, distance)
    if lax.axis_size("fsdp") > 2:
        ahead, behind = ahead + across(left, -distance), behind + across(right, distance)
        total = total + swapped(total, 2)
    parts = jnp.concatenate([total[:RANK, 128:] - ahead, behind - total[RANK:, 128:]], axis=0)
    return jnp.concatenate([total[:, :128], parts], axis=1)


def one_round(tiles, tile, distance, images, held):
    sides = 1 if 2 * distance == lax.axis_size("rep") else 2
    after = along(images, -distance)
    before = after if sides == 1 else along(images, distance)
    leads, keep, send = project(sides, tiles, tile, images, after, before, held)
    total = keep + swapped(send, 1)
    parts = differences(distance, sides, total)
    mine = parts[:, 128:]
    other = swapped(mine, 1)
    inverses, bases = normalise(sides, parts[:, :128], leads)
    return update(sides, tiles, tile, inverses, bases, mine, other, held)


def per_device(query_weights, key_weights, value_weights, query_factor, key_factor, value_factor, step_index):
    weights = (query_weights[0], key_weights[0], value_weights[0])
    levels = lax.axis_size("rep").bit_length() - 1
    tile = min(1024, *[matrix.shape[1] for matrix in weights])
    tiles = tuple(matrix.shape[1] // tile for matrix in weights)
    images, held = images_of(weights, (query_factor, key_factor, value_factor), tiles, tile)
    branches = [functools.partial(one_round, tiles, tile, 1 << level) for level in range(levels)]
    return lax.switch(step_index[0] % levels, branches, images, held)


def solution(mesh):
    split = P("rep", "fsdp", None)
    return jax.shard_map(
        per_device,
        mesh=mesh,
        in_specs=(split, split, split, P(), P(), P(), P()),
        out_specs=(split, split, split) + (P("rep", None, None),) * 3,
        check_vma=False,
    )
```

```python
import functools

import jax
import jax.numpy as jnp
from jax import lax
from jax.experimental import pallas as pl
from jax.experimental.pallas import tpu as pltpu
from jax.sharding import PartitionSpec as P

mixing = 0.25
F32 = jnp.float32
BF16 = jnp.bfloat16
MIB = 2**20
VMEM = pltpu.VMEM
RANK = 8


def vmem_specs(count):
    return [pl.BlockSpec(memory_space=VMEM)] * count


def hbm_specs(count):
    return [pl.BlockSpec(memory_space=pltpu.HBM)] * count


def in_vmem(*arrays):
    return [pltpu.with_memory_space_constraint(array, VMEM) for array in arrays]


def in_hbm(*arrays):
    return [pltpu.with_memory_space_constraint(array, pltpu.HBM) for array in arrays]


def cost(size, rows):
    return pl.CostEstimate(flops=2 * size * rows, bytes_accessed=4 * size, transcendentals=0)


def pieces(value):
    high = value.astype(BF16).astype(F32)
    rest = value - high
    middle = rest.astype(BF16).astype(F32)
    return high, middle, rest - middle


def stack_of(value):
    return jnp.concatenate(pieces(value), axis=0).astype(BF16)


def weight_dot(stacked, weights, contract):
    high = weights.astype(BF16)
    low = (weights - high.astype(F32)).astype(BF16)
    dims = (((1,), (contract,)), ((), ()))
    total = lax.dot_general(stacked, high, dims, preferred_element_type=F32)
    total = total + lax.dot_general(stacked, low, dims, preferred_element_type=F32)
    rows = stacked.shape[0] // 3
    return total[:rows] + total[rows : 2 * rows] + total[2 * rows :]


def family_of(tile, tiles):
    family, place, start = 0, tile, 0
    for count in tiles[:-1]:
        start += count
        family = family + jnp.where(tile >= start, 1, 0)
        place = jnp.where(tile >= start, tile - start, place)
    return family, place


def image_kernel(tiles, tile, block, in_flight, *refs):
    weights, factors = refs[:3], refs[3:6]
    images, held = refs[6:8]
    brought, stack_ref, sems, factor_sems = refs[8:11], refs[11], refs[12], refs[13]
    rows = held.shape[0]
    blocks = rows // block
    jobs = sum(tiles) * blocks

    def copy_of(family, place, job):
        start, wide = (job % blocks) * block, (job // blocks) * tile
        column = place * tile
        if not isinstance(job, int):
            start, wide = pl.multiple_of(start, block), pl.multiple_of(wide, tile)
            column = pl.multiple_of(column, tile)
        source, target = weights[family].at[:, pl.ds(column, tile)], held.at[:, pl.ds(wide, tile)]
        sem = sems.at[job % in_flight]

        def copy(first, count):
            span = pl.ds(start + first, count)
            return pltpu.make_async_copy(source.at[span], target.at[span], sem)

        return copy

    def start_copies(family, place, job, priority):
        copy = copy_of(family, place, job)
        for part in range(4):
            copy(part * (block // 4), block // 4).start(priority=priority)

    for job in range(min(jobs, in_flight)):
        start_copies(0, job // blocks, job, min(job, 1))
    factor_copies = [
        pltpu.make_async_copy(factors[family], brought[family], factor_sems.at[family])
        for family in range(3)
    ]
    for copy in factor_copies:
        copy.start()
    offset = 0
    for family in range(3):
        columns = tiles[family] * tile
        factor_copies[family].wait()
        stack_ref[:, pl.ds(offset, columns)] = stack_of(brought[family][...])
        offset += columns
    images[...] = jnp.zeros_like(images)

    def step(job, carry):
        copy_of(0, 0, job)(0, block).wait()
        following = job + in_flight
        later, place = family_of(following // blocks, tiles)
        for family in range(3):

            @pl.when((later == family) & (following < jobs))
            def _():
                start_copies(family, place, following, 1)

        span = pl.ds(pl.multiple_of((job % blocks) * block, block), block)
        wide = pl.ds(pl.multiple_of((job // blocks) * tile, tile), tile)
        part = weight_dot(stack_ref[:, wide], held[span, wide], 1)
        family, _ = family_of(job // blocks, tiles)
        images[pl.ds(pl.multiple_of(RANK * family, RANK), RANK), span] += part
        return carry

    lax.fori_loop(0, jobs, step, 0)


def images_of(weights, factors, tiles, tile):
    rows = weights[0].shape[0]
    columns = sum(tiles) * tile
    block = min(rows, 1024)
    in_flight = min(2, tiles[0] * (rows // block))
    return pl.pallas_call(
        functools.partial(image_kernel, tiles, tile, block, in_flight),
        out_shape=(jax.ShapeDtypeStruct((3 * RANK, rows), F32), VMEM((rows, columns), F32)),
        in_specs=hbm_specs(6),
        out_specs=tuple(vmem_specs(2)),
        scratch_shapes=[VMEM(factor.shape, F32) for factor in factors]
        + [
            VMEM((3 * RANK, columns), BF16),
            pltpu.SemaphoreType.DMA((in_flight,)),
            pltpu.SemaphoreType.DMA((3,)),
        ],
        compiler_params=pltpu.CompilerParams(vmem_limit_bytes=8 * MIB),
        cost_estimate=cost(rows * columns, RANK),
        name="images",
    )(*in_hbm(*weights, *factors))


def project_half(tiles, tile, part, stack_ref, held, out):
    half = sum(tiles) // 2

    def step(index, carry):
        index = part * half + index
        family, _ = family_of(index, tiles)
        wide = pl.ds(pl.multiple_of(index * tile, tile), tile)
        span = pl.ds(pl.multiple_of(128 + (index % half) * tile, 128), tile)
        out[:, span] = weight_dot(stack_ref[family], held[:, wide], 0)
        return carry

    lax.fori_loop(0, half, step, 0, unroll=3)


def send_kernel(sides, tiles, tile, here, after, before, held, leads, stack_ref, send):
    core = lax.rem(lax.axis_index("fsdp"), 2)
    images = here[...]
    right = images - after[...]
    left = before[...] - images
    rows = RANK * sides
    grams = []
    for family in range(3):
        mine = slice(RANK * family, RANK * family + RANK)
        lead = right[mine] if sides == 1 else jnp.concatenate([right[mine], left[mine]], axis=0)
        leads[pl.ds(rows * family, rows), :] = lead
        stack_ref[family] = stack_of(lead)
        grams.append(
            lax.dot_general(
                lead,
                lead,
                (((1,), (1,)), ((), ())),
                precision=lax.Precision.HIGHEST,
                preferred_element_type=F32,
            )
        )
    send[:, pl.ds(0, 128)] = jnp.concatenate(grams + [jnp.zeros((rows, 128 - 3 * rows), F32)], axis=1)
    project_half(tiles, tile, 1 - core, stack_ref, held, send)


def keep_kernel(tiles, tile, stack_ref, send, held, keep):
    core = lax.rem(lax.axis_index("fsdp"), 2)
    keep[:, pl.ds(0, 128)] = send[:, pl.ds(0, 128)]
    project_half(tiles, tile, core, stack_ref, held, keep)


def project(sides, tiles, tile, here, after, before, held):
    rows = RANK * sides
    width = held.shape[1] // 2 + 128
    params = pltpu.CompilerParams(vmem_limit_bytes=12 * MIB)
    estimate = cost(held.size // 2, 2 * RANK)
    leads, stack, send = pl.pallas_call(
        functools.partial(send_kernel, sides, tiles, tile),
        out_shape=(
            jax.ShapeDtypeStruct((3 * rows, here.shape[1]), F32),
            jax.ShapeDtypeStruct((3, 3 * rows, here.shape[1]), BF16),
            jax.ShapeDtypeStruct((rows, width), F32),
        ),
        in_specs=vmem_specs(4),
        out_specs=tuple(vmem_specs(3)),
        compiler_params=params,
        cost_estimate=estimate,
        name="project_send",
    )(here, after, before, *in_vmem(held))
    keep = pl.pallas_call(
        functools.partial(keep_kernel, tiles, tile),
        out_shape=jax.ShapeDtypeStruct((rows, width), F32),
        in_specs=vmem_specs(3),
        out_specs=vmem_specs(1)[0],
        compiler_params=params,
        cost_estimate=estimate,
        name="project_keep",
    )(stack, send, *in_vmem(held))
    return leads, keep, send


def inverse_cholesky(grams):
    shape = (RANK, RANK)
    row = lax.broadcasted_iota(jnp.int32, shape, 0)
    unit = (row == lax.broadcasted_iota(jnp.int32, shape, 1)).astype(F32)
    tables = [jnp.concatenate([gram, unit], axis=1) for gram in grams]
    below = lax.broadcasted_iota(jnp.int32, (RANK, 1), 0)
    for step in range(RANK):
        after = []
        for table in tables:
            pivot = table[step : step + 1, step : step + 1]
            scale = lax.rsqrt(pivot)
            scale = scale * (1.5 - 0.5 * pivot * scale * scale)
            lead = table[step : step + 1, :] * scale
            factor = table[:, step : step + 1] * scale
            lowered = table - factor * lead
            after.append(jnp.where(below < step, table, jnp.where(below == step, lead, lowered)))
        tables = after
    return [table[:, RANK:] for table in tables]


def apply_rows(matrix, values):
    total = matrix[:, 0:1] * values[0:1, :]
    for index in range(1, RANK):
        total = total + matrix[:, index : index + 1] * values[index : index + 1, :]
    return total


def normalise_kernel(sides, grams, leads, inverses, bases):
    rows = RANK * sides
    tables = []
    for family in range(3):
        for side in range(sides):
            span = slice(RANK * side, RANK * side + RANK)
            start = rows * family + RANK * side
            tables.append(grams[span, start : start + RANK])
    solved = inverse_cholesky(tables)
    for family in range(3):
        basis = []
        for side in range(sides):
            inverse = solved[sides * family + side]
            inverses[family, side] = inverse
            basis.append(apply_rows(inverse, leads[pl.ds(rows * family + RANK * side, RANK), :]))
        high, middle, low = pieces(jnp.concatenate(basis, axis=0) if sides > 1 else basis[0])
        stack = jnp.concatenate([high, high, high, middle, middle, low], axis=0)
        spare = jnp.zeros((128 - stack.shape[0], stack.shape[1]), F32)
        bases[family] = jnp.concatenate([stack, spare], axis=0).T.astype(BF16)


def normalise(sides, grams, leads):
    rows = RANK * sides
    return pl.pallas_call(
        functools.partial(normalise_kernel, sides),
        out_shape=(
            jax.ShapeDtypeStruct((3, sides, RANK, RANK), F32),
            jax.ShapeDtypeStruct((3, leads.shape[1], 128), BF16),
        ),
        in_specs=vmem_specs(2),
        out_specs=tuple(vmem_specs(2)),
        compiler_params=pltpu.CompilerParams(vmem_limit_bytes=4 * MIB),
        cost_estimate=pl.CostEstimate(flops=10**6, bytes_accessed=4 * MIB, transcendentals=48),
        name="normalise",
    )(grams, leads)


def update_kernel(sides, tiles, slots, inverses, bases, mine, other, held, *refs):
    mixed, following = refs[:3], refs[3:6]
    stage, coeff_ref, renewed_ref, sems, small_sems = refs[6:]
    core = lax.rem(lax.axis_index("fsdp"), 2)
    block, tile = stage.shape[1:]
    blocks = held.shape[0] // block
    half = sum(tiles) // 2
    factor = mixing * (2 // sides)

    def copy_of(family, place, job, slot):
        start = pl.multiple_of((job % blocks) * block, block)
        column = pl.multiple_of(place * tile, tile)
        target = mixed[family].at[0, pl.ds(start, block), pl.ds(column, tile)]
        return pltpu.make_async_copy(stage.at[slot], target, sems.at[slot])

    def small_copy(family, place, index):
        wide = pl.ds(pl.multiple_of(place * tile, tile), tile)
        target = following[family].at[0, :, wide]
        return pltpu.make_async_copy(renewed_ref.at[index], target, small_sems.at[index])

    def change(job, carry):
        slot = job % slots
        index = job // blocks
        family, place = family_of(index, tiles)

        @pl.when(job % blocks == 0)
        def _():
            span = pl.ds(pl.multiple_of((index % half) * tile, tile), tile)
            chosen = jnp.where(core == index // half, mine[:, span], other[:, span])
            renewed = [
                apply_rows(inverses[family, side], chosen[RANK * side : RANK * side + RANK])
                for side in range(sides)
            ]
            renewed_ref[index] = renewed[0]
            for which in range(3):

                @pl.when(family == which)
                def _():
                    small_copy(which, place, index).start()

            coeff = renewed[0] if sides == 1 else jnp.concatenate([renewed[0], -renewed[1]], axis=0)
            high, middle, low = pieces(coeff)
            spare = jnp.zeros((128 - 6 * coeff.shape[0], tile), F32)
            stack = jnp.concatenate([high, middle, low, high, middle, high, spare], axis=0)
            coeff_ref[...] = stack.astype(BF16)

        @pl.when(job >= slots)
        def _():
            copy_of(0, 0, 0, slot).wait()

        span = pl.ds(pl.multiple_of((job % blocks) * block, block), block)
        product = jnp.dot(bases[family, span, :], coeff_ref[...], preferred_element_type=F32)
        stage[slot] = held[span, pl.ds(pl.multiple_of(index * tile, tile), tile)] - factor * product
        for which in range(3):

            @pl.when(family == which)
            def _():
                copy_of(which, place, job, slot).start()

        return carry

    jobs = blocks * sum(tiles)
    lax.fori_loop(0, jobs, change, 0)
    for slot in range(min(slots, jobs)):
        copy_of(0, 0, 0, slot).wait()
    for index in range(sum(tiles)):
        small_copy(0, 0, index).wait()


def update(sides, tiles, tile, inverses, bases, mine, other, held):
    rows = held.shape[0]
    slots = 3
    return pl.pallas_call(
        functools.partial(update_kernel, sides, tiles, slots),
        out_shape=tuple(pltpu.HBM((1, rows, count * tile), F32) for count in tiles)
        + tuple(pltpu.HBM((1, RANK, count * tile), F32) for count in tiles),
        in_specs=vmem_specs(5),
        out_specs=tuple(hbm_specs(6)),
        scratch_shapes=[
            VMEM((slots, min(512, rows), tile), F32),
            VMEM((128, tile), BF16),
            VMEM((sum(tiles), RANK, tile), F32),
            pltpu.SemaphoreType.DMA((slots,)),
            pltpu.SemaphoreType.DMA((sum(tiles),)),
        ],
        compiler_params=pltpu.CompilerParams(vmem_limit_bytes=12 * MIB),
        cost_estimate=cost(held.size, 2 * RANK),
        name="update",
    )(inverses, bases, mine, other, *in_vmem(held))


def moved(value, axis, target):
    count = lax.axis_size(axis)
    return lax.ppermute(value, axis, [(source, target(source, count)) for source in range(count)])


def along(value, distance):
    return moved(value, "rep", lambda source, count: (source + distance) % count)


def swapped(value, bit):
    return moved(value, "fsdp", lambda source, count: source ^ bit)


def across(value, distance):
    replicas, count = lax.axis_size("rep"), lax.axis_size("fsdp")
    pairs = [
        (replica * count + place, (replica + distance) % replicas * count + (place ^ 2))
        for replica in range(replicas)
        for place in range(count)
    ]
    return lax.ppermute(value, ("rep", "fsdp"), pairs)


def summed(value, bit):
    while bit < lax.axis_size("fsdp"):
        value = value + swapped(value, bit)
        bit *= 2
    return value


def differences(distance, sides, total):
    if sides == 1:
        right = total[:, 128:]
        return summed(jnp.concatenate([total[:, :128], right + along(right, distance)], axis=1), 2)
    total = summed(total, 4)
    right, left = total[:RANK, 128:], total[RANK:, 128:]
    ahead, behind = along(left, -distance), along(right, distance)
    if lax.axis_size("fsdp") > 2:
        ahead, behind = ahead + across(left, -distance), behind + across(right, distance)
        total = total + swapped(total, 2)
    parts = jnp.concatenate([total[:RANK, 128:] - ahead, behind - total[RANK:, 128:]], axis=0)
    return jnp.concatenate([total[:, :128], parts], axis=1)


def one_round(tiles, tile, distance, images, held):
    sides = 1 if 2 * distance == lax.axis_size("rep") else 2
    after = along(images, -distance)
    before = after if sides == 1 else along(images, distance)
    leads, keep, send = project(sides, tiles, tile, images, after, before, held)
    total = keep + swapped(send, 1)
    parts = differences(distance, sides, total)
    mine = parts[:, 128:]
    other = swapped(mine, 1)
    inverses, bases = normalise(sides, parts[:, :128], leads)
    return update(sides, tiles, tile, inverses, bases, mine, other, held)


def per_device(query_weights, key_weights, value_weights, query_factor, key_factor, value_factor, step_index):
    weights = (query_weights[0], key_weights[0], value_weights[0])
    levels = lax.axis_size("rep").bit_length() - 1
    tile = min(1024, *[matrix.shape[1] for matrix in weights])
    tiles = tuple(matrix.shape[1] // tile for matrix in weights)
    images, held = images_of(weights, (query_factor, key_factor, value_factor), tiles, tile)
    branches = [functools.partial(one_round, tiles, tile, 1 << level) for level in range(levels)]
    return lax.switch(step_index[0] % levels, branches, images, held)


def solution(mesh):
    split = P("rep", "fsdp", None)
    return jax.shard_map(
        per_device,
        mesh=mesh,
        in_specs=(split, split, split, P(), P(), P(), P()),
        out_specs=(split, split, split) + (P("rep", None, None),) * 3,
        check_vma=False,
    )
```

```python
import functools

import jax
import jax.numpy as jnp
from jax import lax
from jax.experimental import pallas as pl
from jax.experimental.pallas import tpu as pltpu
from jax.sharding import PartitionSpec as P

mixing = 0.25
F32 = jnp.float32
BF16 = jnp.bfloat16
MIB = 2**20
VMEM = pltpu.VMEM
RANK = 8


def vmem_specs(count):
    return [pl.BlockSpec(memory_space=VMEM)] * count


def hbm_specs(count):
    return [pl.BlockSpec(memory_space=pltpu.HBM)] * count


def in_vmem(*arrays):
    return [pltpu.with_memory_space_constraint(array, VMEM) for array in arrays]


def in_hbm(*arrays):
    return [pltpu.with_memory_space_constraint(array, pltpu.HBM) for array in arrays]


def cost(size, rows):
    return pl.CostEstimate(flops=2 * size * rows, bytes_accessed=4 * size, transcendentals=0)


def pieces(value):
    high = value.astype(BF16).astype(F32)
    rest = value - high
    middle = rest.astype(BF16).astype(F32)
    return high, middle, rest - middle


def stack_of(value):
    return jnp.concatenate(pieces(value), axis=0).astype(BF16)


def weight_dot(stacked, weights, contract):
    high = weights.astype(BF16)
    low = (weights - high.astype(F32)).astype(BF16)
    dims = (((1,), (contract,)), ((), ()))
    total = lax.dot_general(stacked, high, dims, preferred_element_type=F32)
    total = total + lax.dot_general(stacked, low, dims, preferred_element_type=F32)
    rows = stacked.shape[0] // 3
    return total[:rows] + total[rows : 2 * rows] + total[2 * rows :]


def family_of(tile, tiles):
    family, place, start = 0, tile, 0
    for count in tiles[:-1]:
        start += count
        family = family + jnp.where(tile >= start, 1, 0)
        place = jnp.where(tile >= start, tile - start, place)
    return family, place


def image_kernel(tiles, tile, block, in_flight, *refs):
    weights, factors = refs[:3], refs[3:6]
    images, held = refs[6:8]
    brought, stack_ref, sems, factor_sems = refs[8:11], refs[11], refs[12], refs[13]
    rows = held.shape[0]
    blocks = rows // block
    jobs = sum(tiles) * blocks

    def copy_of(family, place, job):
        start, wide = (job % blocks) * block, (job // blocks) * tile
        column = place * tile
        if not isinstance(job, int):
            start, wide = pl.multiple_of(start, block), pl.multiple_of(wide, tile)
            column = pl.multiple_of(column, tile)
        source, target = weights[family].at[:, pl.ds(column, tile)], held.at[:, pl.ds(wide, tile)]
        sem = sems.at[job % in_flight]

        def copy(first, count):
            span = pl.ds(start + first, count)
            return pltpu.make_async_copy(source.at[span], target.at[span], sem)

        return copy

    def start_copies(family, place, job, priority):
        copy = copy_of(family, place, job)
        for part in range(4):
            copy(part * (block // 4), block // 4).start(priority=priority)

    for job in range(min(jobs, in_flight)):
        start_copies(0, job // blocks, job, min(job, 1))
    factor_copies = [
        pltpu.make_async_copy(factors[family], brought[family], factor_sems.at[family])
        for family in range(3)
    ]
    for copy in factor_copies:
        copy.start()
    offset = 0
    for family in range(3):
        columns = tiles[family] * tile
        factor_copies[family].wait()
        stack_ref[:, pl.ds(offset, columns)] = stack_of(brought[family][...])
        offset += columns
    images[...] = jnp.zeros_like(images)

    def step(job, carry):
        copy_of(0, 0, job)(0, block).wait()
        following = job + in_flight
        later, place = family_of(following // blocks, tiles)
        for family in range(3):

            @pl.when((later == family) & (following < jobs))
            def _():
                start_copies(family, place, following, 1)

        span = pl.ds(pl.multiple_of((job % blocks) * block, block), block)
        wide = pl.ds(pl.multiple_of((job // blocks) * tile, tile), tile)
        part = weight_dot(stack_ref[:, wide], held[span, wide], 1)
        family, _ = family_of(job // blocks, tiles)
        images[pl.ds(pl.multiple_of(RANK * family, RANK), RANK), span] += part
        return carry

    lax.fori_loop(0, jobs, step, 0)


def images_of(weights, factors, tiles, tile):
    rows = weights[0].shape[0]
    columns = sum(tiles) * tile
    block = min(rows, 1024)
    in_flight = min(2, tiles[0] * (rows // block))
    return pl.pallas_call(
        functools.partial(image_kernel, tiles, tile, block, in_flight),
        out_shape=(jax.ShapeDtypeStruct((3 * RANK, rows), F32), VMEM((rows, columns), F32)),
        in_specs=hbm_specs(6),
        out_specs=tuple(vmem_specs(2)),
        scratch_shapes=[VMEM(factor.shape, F32) for factor in factors]
        + [
            VMEM((3 * RANK, columns), BF16),
            pltpu.SemaphoreType.DMA((in_flight,)),
            pltpu.SemaphoreType.DMA((3,)),
        ],
        compiler_params=pltpu.CompilerParams(vmem_limit_bytes=8 * MIB),
        cost_estimate=cost(rows * columns, RANK),
        name="images",
    )(*in_hbm(*weights, *factors))


def project_half(tiles, tile, part, stack_ref, held, out):
    half = sum(tiles) // 2

    def step(index, carry):
        index = part * half + index
        family, _ = family_of(index, tiles)
        wide = pl.ds(pl.multiple_of(index * tile, tile), tile)
        span = pl.ds(pl.multiple_of(128 + (index % half) * tile, 128), tile)
        out[:, span] = weight_dot(stack_ref[family], held[:, wide], 0)
        return carry

    lax.fori_loop(0, half, step, 0, unroll=3)


def send_kernel(sides, tiles, tile, here, after, before, held, leads, stack_ref, send):
    core = lax.rem(lax.axis_index("fsdp"), 2)
    images = here[...]
    right = images - after[...]
    left = before[...] - images
    rows = RANK * sides
    grams = []
    for family in range(3):
        mine = slice(RANK * family, RANK * family + RANK)
        lead = right[mine] if sides == 1 else jnp.concatenate([right[mine], left[mine]], axis=0)
        leads[pl.ds(rows * family, rows), :] = lead
        stack_ref[family] = stack_of(lead)
        grams.append(
            lax.dot_general(
                lead,
                lead,
                (((1,), (1,)), ((), ())),
                precision=lax.Precision.HIGHEST,
                preferred_element_type=F32,
            )
        )
    send[:, pl.ds(0, 128)] = jnp.concatenate(grams + [jnp.zeros((rows, 128 - 3 * rows), F32)], axis=1)
    project_half(tiles, tile, 1 - core, stack_ref, held, send)


def keep_kernel(tiles, tile, stack_ref, send, held, keep):
    core = lax.rem(lax.axis_index("fsdp"), 2)
    keep[:, pl.ds(0, 128)] = send[:, pl.ds(0, 128)]
    project_half(tiles, tile, core, stack_ref, held, keep)


def project(sides, tiles, tile, here, after, before, held):
    rows = RANK * sides
    width = held.shape[1] // 2 + 128
    params = pltpu.CompilerParams(vmem_limit_bytes=12 * MIB)
    estimate = cost(held.size // 2, 2 * RANK)
    leads, stack, send = pl.pallas_call(
        functools.partial(send_kernel, sides, tiles, tile),
        out_shape=(
            jax.ShapeDtypeStruct((3 * rows, here.shape[1]), F32),
            jax.ShapeDtypeStruct((3, 3 * rows, here.shape[1]), BF16),
            jax.ShapeDtypeStruct((rows, width), F32),
        ),
        in_specs=vmem_specs(4),
        out_specs=tuple(vmem_specs(3)),
        compiler_params=params,
        cost_estimate=estimate,
        name="project_send",
    )(here, after, before, *in_vmem(held))
    keep = pl.pallas_call(
        functools.partial(keep_kernel, tiles, tile),
        out_shape=jax.ShapeDtypeStruct((rows, width), F32),
        in_specs=vmem_specs(3),
        out_specs=vmem_specs(1)[0],
        compiler_params=params,
        cost_estimate=estimate,
        name="project_keep",
    )(stack, send, *in_vmem(held))
    return leads, keep, send


def inverse_cholesky(grams):
    shape = (RANK, RANK)
    row = lax.broadcasted_iota(jnp.int32, shape, 0)
    unit = (row == lax.broadcasted_iota(jnp.int32, shape, 1)).astype(F32)
    tables = [jnp.concatenate([gram, unit], axis=1) for gram in grams]
    below = lax.broadcasted_iota(jnp.int32, (RANK, 1), 0)
    for step in range(RANK):
        after = []
        for table in tables:
            pivot = table[step : step + 1, step : step + 1]
            scale = lax.rsqrt(pivot)
            scale = scale * (1.5 - 0.5 * pivot * scale * scale)
            lead = table[step : step + 1, :] * scale
            factor = table[:, step : step + 1] * scale
            lowered = table - factor * lead
            after.append(jnp.where(below < step, table, jnp.where(below == step, lead, lowered)))
        tables = after
    return [table[:, RANK:] for table in tables]


def apply_rows(matrix, values):
    total = matrix[:, 0:1] * values[0:1, :]
    for index in range(1, RANK):
        total = total + matrix[:, index : index + 1] * values[index : index + 1, :]
    return total


def normalise_kernel(sides, grams, leads, inverses, bases):
    rows = RANK * sides
    tables = []
    for family in range(3):
        for side in range(sides):
            span = slice(RANK * side, RANK * side + RANK)
            start = rows * family + RANK * side
            tables.append(grams[span, start : start + RANK])
    solved = inverse_cholesky(tables)
    for family in range(3):
        basis = []
        for side in range(sides):
            inverse = solved[sides * family + side]
            inverses[family, side] = inverse
            basis.append(apply_rows(inverse, leads[pl.ds(rows * family + RANK * side, RANK), :]))
        high, middle, low = pieces(jnp.concatenate(basis, axis=0) if sides > 1 else basis[0])
        stack = jnp.concatenate([high, high, high, middle, middle, low], axis=0)
        spare = jnp.zeros((128 - stack.shape[0], stack.shape[1]), F32)
        bases[family] = jnp.concatenate([stack, spare], axis=0).T.astype(BF16)


def normalise(sides, grams, leads):
    rows = RANK * sides
    return pl.pallas_call(
        functools.partial(normalise_kernel, sides),
        out_shape=(
            jax.ShapeDtypeStruct((3, sides, RANK, RANK), F32),
            jax.ShapeDtypeStruct((3, leads.shape[1], 128), BF16),
        ),
        in_specs=vmem_specs(2),
        out_specs=tuple(vmem_specs(2)),
        compiler_params=pltpu.CompilerParams(vmem_limit_bytes=4 * MIB),
        cost_estimate=pl.CostEstimate(flops=10**6, bytes_accessed=4 * MIB, transcendentals=48),
        name="normalise",
    )(grams, leads)


def update_kernel(sides, tiles, slots, inverses, bases, mine, other, held, *refs):
    mixed, following = refs[:3], refs[3:6]
    stage, coeff_ref, renewed_ref, sems, small_sems = refs[6:]
    core = lax.rem(lax.axis_index("fsdp"), 2)
    block, tile = stage.shape[1:]
    blocks = held.shape[0] // block
    half = sum(tiles) // 2
    factor = mixing * (2 // sides)

    def copy_of(family, place, job, slot):
        start = pl.multiple_of((job % blocks) * block, block)
        column = pl.multiple_of(place * tile, tile)
        target = mixed[family].at[0, pl.ds(start, block), pl.ds(column, tile)]
        return pltpu.make_async_copy(stage.at[slot], target, sems.at[slot])

    def small_copy(family, place, index):
        wide = pl.ds(pl.multiple_of(place * tile, tile), tile)
        target = following[family].at[0, :, wide]
        return pltpu.make_async_copy(renewed_ref.at[index], target, small_sems.at[index])

    def change(index, carry):
        family, place = family_of(index, tiles)
        span = pl.ds(pl.multiple_of((index % half) * tile, tile), tile)
        chosen = jnp.where(core == index // half, mine[:, span], other[:, span])
        renewed = [
            apply_rows(inverses[family, side], chosen[RANK * side : RANK * side + RANK])
            for side in range(sides)
        ]
        renewed_ref[index] = renewed[0]
        coeff = renewed[0] if sides == 1 else jnp.concatenate([renewed[0], -renewed[1]], axis=0)
        high, middle, low = pieces(coeff)
        spare = jnp.zeros((128 - 6 * coeff.shape[0], tile), F32)
        stack = jnp.concatenate([high, middle, low, high, middle, high, spare], axis=0)
        coeff_ref[...] = stack.astype(BF16)
        wide = pl.ds(pl.multiple_of(index * tile, tile), tile)
        for row in range(blocks):
            job = index * blocks + row
            slot = job % slots

            @pl.when(job >= slots)
            def _():
                copy_of(0, 0, 0, slot).wait()

            span = pl.ds(row * block, block)
            product = jnp.dot(bases[family, span, :], coeff_ref[...], preferred_element_type=F32)
            stage[slot] = held[span, wide] - factor * product
            for which in range(3):

                @pl.when(family == which)
                def _():
                    copy_of(which, place, job, slot).start()
                    if row == 0:
                        small_copy(which, place, index).start()

        return carry

    jobs = blocks * sum(tiles)
    lax.fori_loop(0, sum(tiles), change, 0)
    for slot in range(min(slots, jobs)):
        copy_of(0, 0, 0, slot).wait()
    for index in range(sum(tiles)):
        small_copy(0, 0, index).wait()


def update(sides, tiles, tile, inverses, bases, mine, other, held):
    rows = held.shape[0]
    slots = 3
    return pl.pallas_call(
        functools.partial(update_kernel, sides, tiles, slots),
        out_shape=tuple(pltpu.HBM((1, rows, count * tile), F32) for count in tiles)
        + tuple(pltpu.HBM((1, RANK, count * tile), F32) for count in tiles),
        in_specs=vmem_specs(5),
        out_specs=tuple(hbm_specs(6)),
        scratch_shapes=[
            VMEM((slots, min(512, rows), tile), F32),
            VMEM((128, tile), BF16),
            VMEM((sum(tiles), RANK, tile), F32),
            pltpu.SemaphoreType.DMA((slots,)),
            pltpu.SemaphoreType.DMA((sum(tiles),)),
        ],
        compiler_params=pltpu.CompilerParams(vmem_limit_bytes=12 * MIB),
        cost_estimate=cost(held.size, 2 * RANK),
        name="update",
    )(inverses, bases, mine, other, *in_vmem(held))


def moved(value, axis, target):
    count = lax.axis_size(axis)
    return lax.ppermute(value, axis, [(source, target(source, count)) for source in range(count)])


def along(value, distance):
    return moved(value, "rep", lambda source, count: (source + distance) % count)


def swapped(value, bit):
    return moved(value, "fsdp", lambda source, count: source ^ bit)


def across(value, distance):
    replicas, count = lax.axis_size("rep"), lax.axis_size("fsdp")
    pairs = [
        (replica * count + place, (replica + distance) % replicas * count + (place ^ 2))
        for replica in range(replicas)
        for place in range(count)
    ]
    return lax.ppermute(value, ("rep", "fsdp"), pairs)


def summed(value, bit):
    while bit < lax.axis_size("fsdp"):
        value = value + swapped(value, bit)
        bit *= 2
    return value


def differences(distance, sides, total):
    if sides == 1:
        right = total[:, 128:]
        return summed(jnp.concatenate([total[:, :128], right + along(right, distance)], axis=1), 2)
    total = summed(total, 4)
    right, left = total[:RANK, 128:], total[RANK:, 128:]
    ahead, behind = along(left, -distance), along(right, distance)
    if lax.axis_size("fsdp") > 2:
        ahead, behind = ahead + across(left, -distance), behind + across(right, distance)
        total = total + swapped(total, 2)
    parts = jnp.concatenate([total[:RANK, 128:] - ahead, behind - total[RANK:, 128:]], axis=0)
    return jnp.concatenate([total[:, :128], parts], axis=1)


def one_round(tiles, tile, distance, images, held):
    sides = 1 if 2 * distance == lax.axis_size("rep") else 2
    after = along(images, -distance)
    before = after if sides == 1 else along(images, distance)
    leads, keep, send = project(sides, tiles, tile, images, after, before, held)
    total = keep + swapped(send, 1)
    parts = differences(distance, sides, total)
    mine = parts[:, 128:]
    other = swapped(mine, 1)
    inverses, bases = normalise(sides, parts[:, :128], leads)
    return update(sides, tiles, tile, inverses, bases, mine, other, held)


def per_device(query_weights, key_weights, value_weights, query_factor, key_factor, value_factor, step_index):
    weights = (query_weights[0], key_weights[0], value_weights[0])
    levels = lax.axis_size("rep").bit_length() - 1
    tile = min(1024, *[matrix.shape[1] for matrix in weights])
    tiles = tuple(matrix.shape[1] // tile for matrix in weights)
    images, held = images_of(weights, (query_factor, key_factor, value_factor), tiles, tile)
    branches = [functools.partial(one_round, tiles, tile, 1 << level) for level in range(levels)]
    return lax.switch(step_index[0] % levels, branches, images, held)


def solution(mesh):
    split = P("rep", "fsdp", None)
    return jax.shard_map(
        per_device,
        mesh=mesh,
        in_specs=(split, split, split, P(), P(), P(), P()),
        out_specs=(split, split, split) + (P("rep", None, None),) * 3,
        check_vma=False,
    )
```
